256 devices in a mesh: seq: 32 (over x, y, core), exp: 8 (over z).
Axes of the slice: x: 4, y: 4, z: 8, core: 2. Of those that a mesh axis runs over, the one named last changes fastest.
Arguments:
- queries: bfloat16 [4096, 4096], P('seq', 'exp'), may hold values from -135 to 135
- attn_keys: bfloat16 [4096, 512], P('seq', 'exp'), may hold values from -4.5 to 4.5
- attn_values: bfloat16 [4096, 512], P('seq', 'exp'), may hold values from -6 to 6
- sink_logits: float32 [64], P('exp'), may hold values from -1 to 3
- out_proj: bfloat16 [4096, 2880], P('exp'), may hold values from -0.09375 to 0.09375
- residual: bfloat16 [4096, 2880], P('seq', 'exp'), may hold values from -6 to 6
- norm_gain: float32 [2880], replicated, may hold values from 0.5 to 1.5
- doc_start: int32 [4096], P('seq'), may hold values from 0 to 4095, as said below
- expert_ids: int32 [4096, 4], P('seq'), may hold values from 0 to 31, all different within a row; in each aligned block of 128 rows (0 to 127, 128 to 255, ...) at most 32 rows name the same one
- route_scores: float32 [4096, 4], P('seq'), may hold values from 0.2 to 1
- w_gate_up: bfloat16 [32, 2, 2880, 2880], P('seq', None, None, 'exp'), may hold values from -0.109375 to 0.109375
- w_down: bfloat16 [32, 2880, 2880], P('seq', 'exp'), may hold values from -0.109375 to 0.109375
- control: float32 [2880], replicated, may hold values from 0 to 1
Outputs:
- grad_gate_up: bfloat16 [32, 2, 2880, 2880], P('seq', None, None, 'exp')
The draws below stay inside these ranges and needn't reach their ends.
Inputs may be any that keep to these rules, and one draw needn't show every extreme that they name: `expert_ids`: each row names 4 different experts; among the 128 rows of one index of seq no expert is named by more than 32 rows, a bound that some block reaches. doc_start of a position is the first position of its document: never above the position itself, never falling along the pack, equal within a document; position 0 starts a document, and the last position of the pack is a document of its own.
All inputs are finite; a program needn't handle non-finite values.
Results may differ from the reference program's by a relative error of at most 0.0075.
Values may be sent and summed in bfloat16 or wider, within the bound.
No kernel may reach another device: no remote copies, remote signals or barrier semaphores. Data moves between devices by JAX's collectives and lax.ppermute only.
A program may use at most 128 MiB of HBM per device.

```python
import math
import jax
import jax.numpy as jnp
import numpy as np
from jax import lax

D = 2880
HEADS = 64
KV_HEADS = 8
HEAD_DIM = 64
FF = 2880
WINDOW = 128
TOPK = 4
SEG = 128
PACK = 4096
EXPERTS = 32
CAP = 32
HID_BLOCKS = 8
N_SEQ = 32


def paired_rows(key):
    base = jax.random.fold_in(key, 11)
    key_keys, key_queries = jax.random.split(base, 2)
    key_rows = jnp.clip(jax.random.normal(key_keys, (PACK, KV_HEADS * HEAD_DIM), jnp.float32), -4.5, 4.5)
    query_rows = jnp.clip(jax.random.normal(key_queries, (PACK, HEADS * HEAD_DIM), jnp.float32), -4.5, 4.5)
    return (query_rows, key_rows)


def draw_queries(key, part):
    return paired_rows(key)[0].astype(jnp.bfloat16)


def draw_attn_keys(key, part):
    return paired_rows(key)[1].astype(jnp.bfloat16)


def draw_doc_start(key, part):
    folded = jax.random.fold_in(key, 23)
    position = jnp.arange(PACK, dtype=jnp.int32)
    cuts = (jax.random.randint(folded, (PACK,), 0, 2 * SEG) == 0) | (position == 0) | (position == PACK - 1)
    return lax.cummax(jnp.where(cuts, position, 0), axis=0)


def steps_of(key, shape, pieces, smallest, high):
    gain = 1.0
    for axis_at, shards_of in pieces:
        steps = jax.random.uniform(jax.random.fold_in(jax.random.fold_in(key, 6), axis_at), (shards_of,), jnp.float32, smallest / len(pieces), high / len(pieces))
        gain = gain * jnp.repeat(jnp.exp(steps), shape[axis_at] // shards_of).reshape((-1,) + (1,) * (len(shape) - 1 - axis_at))
    return gain


def assign_block(rng, own, number, rows, count, top, reach, slope):
    ranking = jax.random.permutation(rng, count)
    packed, common = shares(count, rows * top, reach, slope, True), shares(count, rows * top, reach, slope, False)
    places = jnp.arange(count)

    def named(lengths, rotation):
        used = int((lengths > 0).sum())
        fixed = max(1, used // 4)
        moved = fixed + (places - fixed + rotation * (used - fixed)) % max(1, count - fixed)
        return jnp.zeros((count,), jnp.int32).at[ranking[jnp.where(places < fixed, places, moved)]].set(jnp.asarray(lengths, jnp.int32))

    lengths = jnp.where(number % 4 == 0, named(packed, number // 4), named(common, number - number // 4 - 1))
    mixed = jax.random.permutation(jax.random.fold_in(own, 3), count)
    source_of, sink = mixed[0:count // 2 * 2:2], mixed[1:count // 2 * 2:2]
    margin = jnp.minimum(lengths[source_of] - 1, reach - lengths[sink]) // 2
    margin = jnp.where((source_of == ranking[0]) | (sink == ranking[0]) | (lengths[sink] == 0), 0, jnp.maximum(margin, 0))
    moved = jax.random.randint(jax.random.fold_in(own, 4), (count // 2,), 0, 1 << 20) % (margin + 1)
    lengths = lengths.at[source_of].add(-moved).at[sink].add(moved)
    items = jnp.searchsorted(jnp.cumsum(lengths), jnp.arange(rows * top), side="right").astype(jnp.int32)
    grid = items.reshape(top, rows).T
    grid = grid[jax.random.permutation(jax.random.fold_in(own, 1), rows)]
    rotation = jax.random.randint(jax.random.fold_in(own, 2), (rows, 1), 0, top)
    return jnp.take_along_axis(grid, (jnp.arange(top)[None, :] + rotation) % top, axis=1)


def shares(number_of, total, reach, skew, full):
    portions = [(1 << 20) // math.isqrt(standing ** skew) + 1 for standing in range(1, number_of + 1)]
    largest = reach if full else min(reach, max(-(-total // number_of), total * portions[0] // sum(portions)))
    least = 1 if total - largest >= number_of - 1 else 0
    holding, spare = [largest] + [least] * (number_of - 1), total - largest - least * (number_of - 1)
    while spare > 0:
        movable = [i for i in range(1, number_of) if holding[i] < largest] or [i for i in range(1, number_of) if holding[i] < reach]
        mass, budget = sum([portions[i] for i in movable]), spare
        for i in movable:
            extra = min(reach - holding[i], max(1, budget * portions[i] // mass), spare)
            holding[i] = holding[i] + extra
            spare = spare - extra
    return np.array(holding)


def scatter_about(stream_key, dims, deviation, most, pieces=(), kind=jnp.bfloat16):
    gain = steps_of(stream_key, dims, pieces, -0.22, 0.18) if pieces else 1.0
    array = jax.random.normal(stream_key, dims, jnp.float32) * deviation * gain
    return jnp.minimum(jnp.maximum(array, -most), most).astype(kind)


def setup_inputs(seed: int = 0) -> dict:
    splits = jax.random.split(jax.random.key(seed), 14)
    queries = draw_queries(jax.random.fold_in(splits[13], 71), 0)
    attn_keys = draw_attn_keys(jax.random.fold_in(splits[13], 71), 0)
    attn_values = scatter_about(splits[2], (PACK, KV_HEADS * HEAD_DIM), 1.0, 6.0, ((0, 32), (1, 8)))
    sink_logits = jnp.clip(-1.0 + 4.0 * jax.random.uniform(splits[3], (HEADS,), jnp.float32) ** steps_of(splits[3], (HEADS,), ((0, 8),), -0.2, 0.2), -1.0, 3.0)
    out_proj = scatter_about(splits[4], (HEADS * HEAD_DIM, D), (HEADS * HEAD_DIM) ** -0.5, 0.09375, ((0, 8),))
    residual = scatter_about(splits[5], (PACK, D), 1.0, 6.0, ((0, 32), (1, 8)))
    norm_gain = jnp.clip(1.0 + 0.1 * jax.random.normal(splits[6], (D,), jnp.float32), 0.5, 1.5)
    doc_start = draw_doc_start(jax.random.fold_in(splits[13], 71), 0)
    expert_ids_keys = jax.random.split(jax.random.fold_in(splits[8], 1), PACK // SEG)
    expert_ids_turns = jax.random.permutation(jax.random.fold_in(splits[8], 3), PACK // SEG)
    expert_ids = jax.vmap(lambda own, number: assign_block(jax.random.fold_in(splits[8], 2), own, number, SEG, EXPERTS, TOPK, CAP, 1))(expert_ids_keys, expert_ids_turns).reshape((PACK, TOPK))
    route_scores = jnp.clip(0.2 + 0.8 * jax.random.uniform(splits[9], (PACK, TOPK), jnp.float32) ** steps_of(splits[9], (PACK, TOPK), ((0, 32),), -0.2, 0.2), 0.2, 1.0)
    w_gate_up = scatter_about(splits[10], (EXPERTS, 2, D, FF), D ** -0.5, 0.109375, ((0, 32), (3, 8)))
    w_down = scatter_about(splits[11], (EXPERTS, FF, D), FF ** -0.5, 0.109375, ((0, 32), (1, 8)))
    control = jnp.clip(jax.random.uniform(splits[12], (D,), jnp.float32, 0.0, 1.0), 0.0, 1.0)
    return {"queries": queries, "attn_keys": attn_keys, "attn_values": attn_values, "sink_logits": sink_logits, "out_proj": out_proj, "residual": residual, "norm_gain": norm_gain, "doc_start": doc_start, "expert_ids": expert_ids, "route_scores": route_scores, "w_gate_up": w_gate_up, "w_down": w_down, "control": control}


GLU_ALPHA = 1.702
STEER = 6.5
EPSILON = 1e-05
MASKED = -1e+30

def attend(query_rows, keys_all, values_all, sink_logits, starts, query_pos, key_pos):
    group_size = HEADS // KV_HEADS
    allowed = (key_pos[None, :] <= query_pos[:, None]) & (key_pos[None, :] > query_pos[:, None] - WINDOW) & (key_pos[None, :] >= starts[:, None])
    grouped = query_rows.reshape(SEG, KV_HEADS, group_size, HEAD_DIM).astype(jnp.float32)
    keys_grid = keys_all.reshape(SEG + WINDOW, KV_HEADS, HEAD_DIM).astype(jnp.float32)
    values_grid = values_all.reshape(SEG + WINDOW, KV_HEADS, HEAD_DIM).astype(jnp.float32)
    scores = jnp.einsum('qcgd,kcd->cgqk', grouped, keys_grid) * HEAD_DIM ** (-0.5)
    masked_scores = jnp.where(allowed[None, None], scores, MASKED)
    sink_grid = sink_logits.reshape(KV_HEADS, group_size, 1, 1)
    row_top = jnp.maximum(lax.optimization_barrier(jnp.max(masked_scores, axis=-1, keepdims=True)), sink_grid)
    expo_scores = jnp.where(allowed[None, None], jnp.exp(masked_scores - row_top), 0.0)
    denominator = lax.optimization_barrier(jnp.sum(expo_scores, axis=-1, keepdims=True)) + jnp.exp(sink_grid - row_top)
    attn_weights = (expo_scores / denominator).astype(jnp.bfloat16)
    mixed_heads = jnp.einsum('cgqk,kcd->qcgd', attn_weights.astype(jnp.float32), values_grid)
    return mixed_heads.astype(jnp.bfloat16).reshape(SEG, HEADS * HEAD_DIM)

def reference(queries, attn_keys, attn_values, sink_logits, out_proj, residual, norm_gain, doc_start, expert_ids, route_scores, w_gate_up, w_down, control):
    zero_rim = jnp.zeros((WINDOW, KV_HEADS * HEAD_DIM), attn_keys.dtype)
    keys_padded = jnp.concatenate([zero_rim, attn_keys], axis=0)
    values_padded = jnp.concatenate([zero_rim, attn_values], axis=0)

    def one_block(number):
        offset = (number * SEG).astype(jnp.int32)
        query_rows = lax.dynamic_slice_in_dim(queries, offset, SEG, 0)
        keys_all = lax.dynamic_slice_in_dim(keys_padded, offset, SEG + WINDOW, 0)
        values_all = lax.dynamic_slice_in_dim(values_padded, offset, SEG + WINDOW, 0)
        starts = lax.dynamic_slice_in_dim(doc_start, offset, SEG, 0)
        query_pos = offset + jnp.arange(SEG, dtype=jnp.int32)
        key_pos = offset - WINDOW + jnp.arange(SEG + WINDOW, dtype=jnp.int32)
        return attend(query_rows, keys_all, values_all, sink_logits, starts, query_pos, key_pos)
    heads_out = lax.map(one_block, jnp.arange(N_SEQ, dtype=jnp.int32)).reshape(PACK, HEADS * HEAD_DIM)
    mixed = residual.astype(jnp.float32) + jnp.dot(heads_out, out_proj, preferred_element_type=jnp.float32)
    normed = (mixed * lax.rsqrt(lax.optimization_barrier(jnp.mean(mixed * mixed, axis=-1, keepdims=True)) + EPSILON) * norm_gain).astype(jnp.bfloat16)
    route_gates = route_scores / lax.optimization_barrier(jnp.sum(route_scores, axis=-1, keepdims=True))
    rows_max = N_SEQ * CAP
    block_width = FF // HID_BLOCKS

    def select(expert):
        member = expert_ids == expert
        weight_row = lax.optimization_barrier(jnp.sum(jnp.where(member, route_gates, 0.0), axis=1))
        routed = jnp.any(member, axis=1)
        count = jnp.sum(routed.astype(jnp.int32))
        picks = jnp.nonzero(routed, size=rows_max, fill_value=0)[0].astype(jnp.int32)
        live = jnp.arange(rows_max, dtype=jnp.int32) < count
        weight_live = jnp.where(live, weight_row[picks], 0.0)
        return (picks, weight_live)

    def expert_front(expert, picks):
        rows = normed[picks]
        gate_value = jnp.dot(rows, w_gate_up[expert, 0], preferred_element_type=jnp.float32)
        up_value = jnp.dot(rows, w_gate_up[expert, 1], preferred_element_type=jnp.float32)
        return (rows, gate_value, up_value)

    def forward(moe_out, expert):
        picks, weight_live = select(expert)
        rows, gate_value, up_value = expert_front(expert, picks)
        squashed = jax.nn.sigmoid(GLU_ALPHA * gate_value)
        hidden = ((up_value + 1.0) * gate_value * squashed).astype(jnp.bfloat16)
        blocks = hidden.reshape(rows_max, HID_BLOCKS, block_width).astype(jnp.float32)
        down_blocks = w_down[expert].reshape(HID_BLOCKS, block_width, D).astype(jnp.float32)
        block_out = jnp.einsum('rbf,bfd->brd', blocks, down_blocks).astype(jnp.bfloat16)
        block_out = lax.optimization_barrier(block_out)
        summed = lax.optimization_barrier(jnp.sum(block_out.astype(jnp.float32), axis=0))
        return (moe_out.at[picks].add(weight_live[:, None] * summed), None)
    moe_out, _ = lax.scan(forward, jnp.zeros((PACK, D), jnp.float32), jnp.arange(EXPERTS, dtype=jnp.int32))
    target = STEER * control / jnp.sqrt(jnp.sum(control * control))
    residual_error = mixed + moe_out - target[None, :]

    def backward(carry, expert):
        picks, weight_live = select(expert)
        rows, gate_value, up_value = expert_front(expert, picks)
        squashed = jax.nn.sigmoid(GLU_ALPHA * gate_value)
        d_out = (weight_live[:, None] * residual_error[picks]).astype(jnp.bfloat16)
        d_hidden = jnp.dot(d_out, w_down[expert].T, preferred_element_type=jnp.float32)
        d_gate = (d_hidden * (up_value + 1.0) * (squashed + GLU_ALPHA * gate_value * squashed * (1.0 - squashed))).astype(jnp.bfloat16)
        d_up = (d_hidden * gate_value * squashed).astype(jnp.bfloat16)
        grad_gate = jnp.dot(rows.T, d_gate, preferred_element_type=jnp.float32)
        grad_up = jnp.dot(rows.T, d_up, preferred_element_type=jnp.float32)
        return (carry, jnp.stack([grad_gate, grad_up]).astype(jnp.bfloat16))
    _, grads = lax.scan(backward, jnp.zeros((), jnp.float32), jnp.arange(EXPERTS, dtype=jnp.int32))
    return grads
```

```python
import jax
import jax.numpy as jnp
from jax import lax
from jax.sharding import PartitionSpec as P

HEAD_DIM = 64
WINDOW = 128
TOPK = 4
GLU_ALPHA = 1.702
STEER = 6.5
EPSILON = 1e-05
MASKED = -1e30
BF16 = jnp.bfloat16
F32 = jnp.float32


def passed_along(block, axis, distance):
    devices = range(lax.axis_size(axis))
    route = [(i - distance, i) for i in devices if i - distance in devices]
    return lax.ppermute(block, axis, route)


def attend(queries, attn_keys, attn_values, sink_logits, doc_start):
    seg_len = queries.shape[0]
    heads_here = queries.shape[1] // HEAD_DIM
    kv_here = attn_keys.shape[1] // HEAD_DIM
    group_size = heads_here // kv_here
    both_rims = passed_along(jnp.stack([attn_keys, attn_values]), "seq", 1)
    keys_all = jnp.concatenate([both_rims[0], attn_keys], axis=0).reshape(
        WINDOW + seg_len, kv_here, HEAD_DIM
    )
    values_all = jnp.concatenate([both_rims[1], attn_values], axis=0).reshape(
        WINDOW + seg_len, kv_here, HEAD_DIM
    )
    offset = lax.axis_index("seq") * seg_len
    query_pos = offset + jnp.arange(seg_len, dtype=jnp.int32)
    key_pos = offset - WINDOW + jnp.arange(WINDOW + seg_len, dtype=jnp.int32)
    allowed = (
        (key_pos[None, :] <= query_pos[:, None])
        & (key_pos[None, :] > query_pos[:, None] - WINDOW)
        & (key_pos[None, :] >= doc_start[:, None])
    )
    grouped = queries.reshape(seg_len, kv_here, group_size, HEAD_DIM)
    scores = jnp.einsum(
        "qcgd,kcd->cgqk", grouped, keys_all, preferred_element_type=F32
    ) * HEAD_DIM ** (-0.5)
    masked_scores = jnp.where(allowed[None, None], scores, MASKED)
    sink_grid = sink_logits.reshape(kv_here, group_size, 1, 1)
    row_top = jnp.maximum(jnp.max(masked_scores, axis=-1, keepdims=True), sink_grid)
    expo_scores = jnp.where(allowed[None, None], jnp.exp(masked_scores - row_top), 0.0)
    denominator = jnp.sum(expo_scores, axis=-1, keepdims=True) + jnp.exp(sink_grid - row_top)
    attn_weights = (expo_scores / denominator).astype(BF16)
    mixed_heads = jnp.einsum(
        "cgqk,kcd->qcgd", attn_weights, values_all, preferred_element_type=F32
    )
    return mixed_heads.astype(BF16).reshape(seg_len, heads_here * HEAD_DIM)


def up_ring(block):
    n = lax.axis_size("exp")
    return lax.ppermute(block, "exp", [(i, (i + 1) % n) for i in range(n)])


def down_ring(block):
    n = lax.axis_size("exp")
    return lax.ppermute(block, "exp", [(i, (i - 1) % n) for i in range(n)])


def ring_sum(part_for):
    n = lax.axis_size("exp")
    far = n // 2
    ahead = up_ring(part_for(far, 0).astype(BF16)).astype(F32)
    behind = down_ring(part_for(far, 1).astype(BF16)).astype(F32)
    rows = ahead.shape[0]
    for distance in range(far - 1, 0, -1):
        if distance == far - 1:
            ahead = jnp.pad(ahead, ((0, rows), (0, 0)))
            behind = jnp.pad(behind, ((rows, 0), (0, 0)))
        ahead = up_ring((part_for(distance, None) + ahead).astype(BF16)).astype(F32)
        behind = down_ring((part_for(-distance, None) + behind).astype(BF16)).astype(F32)
    return part_for(0, None) + ahead + behind


def ring_visit(own, visit):
    n = lax.axis_size("exp")
    far = n // 2
    ahead = behind = own
    visit(0, own)
    for distance in range(1, far):
        ahead = up_ring(ahead)
        behind = down_ring(behind)
        visit(-distance, ahead)
        visit(distance, behind)
    rows = own.shape[0] // 2
    ahead = up_ring(ahead[:rows])
    behind = down_ring(behind[rows:])
    visit(far, jnp.concatenate([ahead, behind], axis=0))


def over_seq(rows):
    n_seq = lax.axis_size("seq")
    blocks = rows.reshape(n_seq, rows.shape[0] // n_seq, rows.shape[1])
    return lax.all_to_all(blocks, "seq", split_axis=0, concat_axis=0, tiled=True).reshape(
        rows.shape
    )


def in_pieces(column):
    first = column.astype(BF16)
    second = (column - first.astype(F32)).astype(BF16)
    third = (column - first.astype(F32) - second.astype(F32)).astype(BF16)
    return [first, second, third]


def shards(
    queries,
    attn_keys,
    attn_values,
    sink_logits,
    out_proj,
    residual,
    norm_gain,
    doc_start,
    expert_ids,
    route_scores,
    w_gate_up,
    w_down,
    control,
):
    n_seq = lax.axis_size("seq")
    n_exp = lax.axis_size("exp")
    seg_len, width = residual.shape
    model = out_proj.shape[1]
    hid = w_down.shape[1]
    capacity = 2 * TOPK * seg_len // n_seq
    slots = n_seq * capacity
    me = lax.axis_index("exp")

    def chunk_at(distance):
        return lax.rem(me + distance + n_exp, n_exp)

    def pick(stacked, distance):
        return lax.dynamic_index_in_dim(stacked, chunk_at(distance), 0, keepdims=False)

    heads_out = attend(queries, attn_keys, attn_values, sink_logits, doc_start)
    partial_value = jnp.dot(heads_out, out_proj, preferred_element_type=F32).astype(BF16)
    partial_chunks = partial_value.reshape(seg_len, n_exp, width).transpose(1, 0, 2)

    def mixed_part(distance, half):
        chunk = pick(partial_chunks, distance).astype(F32)
        rows = seg_len // 2
        return chunk if half is None else chunk[half * rows : (half + 1) * rows]

    mixed = ring_sum(mixed_part) + residual.astype(F32)

    experts = jnp.arange(n_seq, dtype=jnp.int32)
    named = expert_ids[:, :, None] == experts[None, None, :]
    member = jnp.any(named, axis=1)
    route_gates = route_scores / jnp.sum(route_scores, axis=-1, keepdims=True)
    gate_table = jnp.sum(jnp.where(named, route_gates[:, :, None], 0.0), axis=1)
    position = jnp.arange(seg_len, dtype=jnp.int32)
    earlier = (position[:, None] > position[None, :]).astype(BF16)
    rank = jnp.dot(earlier, member.astype(BF16), preferred_element_type=F32)
    place = jnp.where(member, rank + 1.0, 0.0).astype(BF16)
    slot = jnp.arange(slots, dtype=jnp.int32)
    spread = (slot[None, :] // capacity == experts[:, None]).astype(BF16)
    place_wide = jnp.dot(place, spread, preferred_element_type=F32)
    taken = (place_wide == (slot % capacity + 1).astype(F32)[None, :]).astype(BF16)
    gate_wide = jnp.dot(gate_table, spread.astype(F32), precision=lax.Precision.HIGHEST)
    gate_slot = jnp.sum(taken.astype(F32) * gate_wide, axis=0)

    def to_slots(rows):
        return lax.dot_general(
            taken, rows, (((0,), (0,)), ((), ())), preferred_element_type=F32
        ).astype(BF16)

    gain = lax.dynamic_slice_in_dim(norm_gain, me * width, width, 0)
    squares = jnp.sum(mixed * mixed, axis=1, keepdims=True)
    payload = jnp.concatenate([(mixed * gain[None, :]).astype(BF16)] + in_pieces(squares), axis=1)
    sent = jnp.concatenate(
        [to_slots(payload)] + in_pieces(gate_slot[:, None]), axis=1
    )
    own_rows = over_seq(sent)
    gates = jnp.sum(own_rows[:, width + 3 : width + 6].astype(F32), axis=1, keepdims=True)

    gate_stack = w_gate_up[0, 0].reshape(n_exp, width, hid)
    up_stack = w_gate_up[0, 1].reshape(n_exp, width, hid)
    down_stack = w_down[0].reshape(hid, n_exp, width).transpose(1, 0, 2)

    state = {
        "rows": jnp.zeros((n_exp, slots, width), BF16),
        "gate": jnp.zeros((slots, hid), F32),
        "up": jnp.zeros((slots, hid), F32),
        "squares": jnp.zeros((slots, 1), F32),
    }

    def front(distance, chunk):
        rows = chunk[:, :width]
        state["rows"] = lax.dynamic_update_index_in_dim(
            state["rows"], rows, chunk_at(distance), 0
        )
        state["gate"] = state["gate"] + jnp.dot(
            rows, pick(gate_stack, distance), preferred_element_type=F32
        )
        state["up"] = state["up"] + jnp.dot(
            rows, pick(up_stack, distance), preferred_element_type=F32
        )
        state["squares"] = state["squares"] + jnp.sum(
            chunk[:, width : width + 3].astype(F32), axis=1, keepdims=True
        )

    ring_visit(own_rows, front)
    scale = lax.rsqrt(state["squares"] / model + EPSILON)
    gate_value = scale * state["gate"]
    up_value = scale * state["up"]
    squashed = jax.nn.sigmoid(GLU_ALPHA * gate_value)
    glu_value = gate_value * squashed
    hidden = (gates * ((up_value + 1.0) * glu_value)).astype(BF16)

    def out_part(distance, half):
        rows = slots // 2
        left = hidden if half is None else hidden[half * rows : (half + 1) * rows]
        return jnp.dot(left, pick(down_stack, distance), preferred_element_type=F32)

    returned = over_seq(ring_sum(out_part).astype(BF16))
    moe_out = jnp.dot(taken, returned, preferred_element_type=F32)
    target = STEER * control / jnp.sqrt(jnp.sum(control * control))
    own_target = lax.dynamic_slice_in_dim(target, me * width, width, 0)
    residual_error = (mixed + moe_out - own_target[None, :]).astype(BF16)

    back = {"hidden": jnp.zeros((slots, hid), F32)}

    def backward(distance, chunk):
        back["hidden"] = back["hidden"] + lax.dot_general(
            chunk,
            pick(down_stack, distance),
            (((1,), (1,)), ((), ())),
            preferred_element_type=F32,
        )

    ring_visit(over_seq(to_slots(residual_error)), backward)
    d_hidden = (gates * scale) * back["hidden"]
    d_gate = (
        d_hidden
        * (up_value + 1.0)
        * (squashed + GLU_ALPHA * gate_value * squashed * (1.0 - squashed))
    ).astype(BF16)
    d_up = (d_hidden * glu_value).astype(BF16)

    def grad(d_value):
        return lax.dot_general(
            state["rows"], d_value, (((1,), (0,)), ((), ())), preferred_element_type=F32
        ).astype(BF16).reshape(model, hid)

    return jnp.stack([grad(d_gate), grad(d_up)])[None]


def solution(mesh):
    return jax.shard_map(
        shards,
        mesh=mesh,
        in_specs=(
            P("seq", "exp"),
            P("seq", "exp"),
            P("seq", "exp"),
            P("exp"),
            P("exp", None),
            P("seq", "exp"),
            P(),
            P("seq"),
            P("seq", None),
            P("seq", None),
            P("seq", None, None, "exp"),
            P("seq", "exp", None),
            P(),
        ),
        out_specs=P("seq", None, None, "exp"),
        check_vma=False,
    )
```

```python
import jax
import jax.numpy as jnp
from jax import lax
from jax.sharding import PartitionSpec as P

HEAD_DIM = 64
WINDOW = 128
TOPK = 4
GLU_ALPHA = 1.702
STEER = 6.5
EPSILON = 1e-05
MASKED = -1e30
BF16 = jnp.bfloat16
F32 = jnp.float32


def passed_along(block, axis, distance):
    devices = range(lax.axis_size(axis))
    route = [(i - distance, i) for i in devices if i - distance in devices]
    return lax.ppermute(block, axis, route)


def attend(queries, attn_keys, attn_values, sink_logits, doc_start):
    seg_len = queries.shape[0]
    heads_here = queries.shape[1] // HEAD_DIM
    kv_here = attn_keys.shape[1] // HEAD_DIM
    group_size = heads_here // kv_here
    both_rims = passed_along(jnp.stack([attn_keys, attn_values]), "seq", 1)
    keys_all = jnp.concatenate([both_rims[0], attn_keys], axis=0).reshape(
        WINDOW + seg_len, kv_here, HEAD_DIM
    )
    values_all = jnp.concatenate([both_rims[1], attn_values], axis=0).reshape(
        WINDOW + seg_len, kv_here, HEAD_DIM
    )
    offset = lax.axis_index("seq") * seg_len
    query_pos = offset + jnp.arange(seg_len, dtype=jnp.int32)
    key_pos = offset - WINDOW + jnp.arange(WINDOW + seg_len, dtype=jnp.int32)
    allowed = (
        (key_pos[None, :] <= query_pos[:, None])
        & (key_pos[None, :] > query_pos[:, None] - WINDOW)
        & (key_pos[None, :] >= doc_start[:, None])
    )
    grouped = queries.reshape(seg_len, kv_here, group_size, HEAD_DIM)
    scores = jnp.einsum(
        "qcgd,kcd->cgqk", grouped, keys_all, preferred_element_type=F32
    ) * HEAD_DIM ** (-0.5)
    masked_scores = jnp.where(allowed[None, None], scores, MASKED)
    sink_grid = sink_logits.reshape(kv_here, group_size, 1, 1)
    row_top = jnp.maximum(jnp.max(masked_scores, axis=-1, keepdims=True), sink_grid)
    expo_scores = jnp.where(allowed[None, None], jnp.exp(masked_scores - row_top), 0.0)
    denominator = jnp.sum(expo_scores, axis=-1, keepdims=True) + jnp.exp(sink_grid - row_top)
    attn_weights = (expo_scores / denominator).astype(BF16)
    mixed_heads = jnp.einsum(
        "cgqk,kcd->qcgd", attn_weights, values_all, preferred_element_type=F32
    )
    return mixed_heads.astype(BF16).reshape(seg_len, heads_here * HEAD_DIM)


def up_ring(block):
    n = lax.axis_size("exp")
    return lax.ppermute(block, "exp", [(i, (i + 1) % n) for i in range(n)])


def down_ring(block):
    n = lax.axis_size("exp")
    return lax.ppermute(block, "exp", [(i, (i - 1) % n) for i in range(n)])


def ring_sum(part_for):
    n = lax.axis_size("exp")
    far = n // 2
    ahead = up_ring(part_for(far, 0).astype(BF16)).astype(F32)
    behind = down_ring(part_for(far, 1).astype(BF16)).astype(F32)
    rows = ahead.shape[0]
    for distance in range(far - 1, 0, -1):
        if distance == far - 1:
            ahead = jnp.pad(ahead, ((0, rows), (0, 0)))
            behind = jnp.pad(behind, ((rows, 0), (0, 0)))
        ahead = up_ring((part_for(distance, None) + ahead).astype(BF16)).astype(F32)
        behind = down_ring((part_for(-distance, None) + behind).astype(BF16)).astype(F32)
    return part_for(0, None) + ahead + behind


def direct_sum(part_for, held):
    n = lax.axis_size("exp")
    arrived = []
    for distance in range(1, n):
        route = [(i, (i + distance) % n) for i in range(n)]
        arrived.append(lax.ppermute(part_for(distance), "exp", route))
        if distance == n // 2:
            arrived, held = lax.optimization_barrier((arrived, held))
    total = part_for(0).astype(F32)
    for share in arrived:
        total = total + share.astype(F32)
    return total, held


def ring_visit(own, visit):
    n = lax.axis_size("exp")
    far = n // 2
    ahead = behind = own
    visit(0, own)
    for distance in range(1, far):
        ahead = up_ring(ahead)
        behind = down_ring(behind)
        visit(-distance, ahead)
        visit(distance, behind)
    rows = own.shape[0] // 2
    ahead = up_ring(ahead[:rows])
    behind = down_ring(behind[rows:])
    visit(far, jnp.concatenate([ahead, behind], axis=0))


def over_seq(rows):
    n_seq = lax.axis_size("seq")
    blocks = rows.reshape(n_seq, rows.shape[0] // n_seq, rows.shape[1])
    return lax.all_to_all(blocks, "seq", split_axis=0, concat_axis=0, tiled=True).reshape(
        rows.shape
    )


def in_pieces(column):
    first = column.astype(BF16)
    second = (column - first.astype(F32)).astype(BF16)
    third = (column - first.astype(F32) - second.astype(F32)).astype(BF16)
    return [first, second, third]


def shards(
    queries,
    attn_keys,
    attn_values,
    sink_logits,
    out_proj,
    residual,
    norm_gain,
    doc_start,
    expert_ids,
    route_scores,
    w_gate_up,
    w_down,
    control,
):
    n_seq = lax.axis_size("seq")
    n_exp = lax.axis_size("exp")
    seg_len, width = residual.shape
    model = out_proj.shape[1]
    hid = w_down.shape[1]
    capacity = 2 * TOPK * seg_len // n_seq
    slots = n_seq * capacity
    me = lax.axis_index("exp")

    def chunk_at(distance):
        return lax.rem(me + distance + n_exp, n_exp)

    def pick(stacked, distance):
        return lax.dynamic_index_in_dim(stacked, chunk_at(distance), 0, keepdims=False)

    heads_out = attend(queries, attn_keys, attn_values, sink_logits, doc_start)
    partial_value = jnp.dot(heads_out, out_proj, preferred_element_type=F32).astype(BF16)
    partial_chunks = partial_value.reshape(seg_len, n_exp, width).transpose(1, 0, 2)

    stacks = [
        w_gate_up[0, 0].reshape(n_exp, width, hid),
        w_gate_up[0, 1].reshape(n_exp, width, hid),
        w_down[0].reshape(hid, n_exp, width).transpose(1, 0, 2),
    ]
    own_sum, stacks = direct_sum(lambda distance: pick(partial_chunks, distance), stacks)
    gate_stack, up_stack, down_stack = stacks
    mixed = own_sum + residual.astype(F32)

    experts = jnp.arange(n_seq, dtype=jnp.int32)
    named = expert_ids[:, :, None] == experts[None, None, :]
    member = jnp.any(named, axis=1)
    route_gates = route_scores / jnp.sum(route_scores, axis=-1, keepdims=True)
    gate_table = jnp.sum(jnp.where(named, route_gates[:, :, None], 0.0), axis=1)
    position = jnp.arange(seg_len, dtype=jnp.int32)
    earlier = (position[:, None] > position[None, :]).astype(BF16)
    rank = jnp.dot(earlier, member.astype(BF16), preferred_element_type=F32)
    place = jnp.where(member, rank + 1.0, 0.0).astype(BF16)
    slot = jnp.arange(slots, dtype=jnp.int32)
    spread = (slot[None, :] // capacity == experts[:, None]).astype(BF16)
    place_wide = jnp.dot(place, spread, preferred_element_type=F32)
    taken = (place_wide == (slot % capacity + 1).astype(F32)[None, :]).astype(BF16)
    gate_wide = jnp.dot(gate_table, spread.astype(F32), precision=lax.Precision.HIGHEST)
    gate_slot = jnp.sum(taken.astype(F32) * gate_wide, axis=0)

    def to_slots(rows):
        return lax.dot_general(
            taken, rows, (((0,), (0,)), ((), ())), preferred_element_type=F32
        ).astype(BF16)

    gain = lax.dynamic_slice_in_dim(norm_gain, me * width, width, 0)
    squares = jnp.sum(mixed * mixed, axis=1, keepdims=True)
    payload = jnp.concatenate([(mixed * gain[None, :]).astype(BF16)] + in_pieces(squares), axis=1)
    sent = jnp.concatenate(
        [to_slots(payload)] + in_pieces(gate_slot[:, None]), axis=1
    )
    own_rows = over_seq(sent)
    gates = jnp.sum(own_rows[:, width + 3 : width + 6].astype(F32), axis=1, keepdims=True)

    state = {
        "rows": jnp.zeros((model, slots), BF16),
        "gate": jnp.zeros((slots, hid), F32),
        "up": jnp.zeros((slots, hid), F32),
        "squares": jnp.zeros((slots, 1), F32),
    }

    def front(distance, chunk):
        rows = chunk[:, :width]
        state["rows"] = lax.dynamic_update_slice_in_dim(
            state["rows"], rows.T, chunk_at(distance) * width, 0
        )
        state["gate"] = state["gate"] + jnp.dot(
            rows, pick(gate_stack, distance), preferred_element_type=F32
        )
        state["up"] = state["up"] + jnp.dot(
            rows, pick(up_stack, distance), preferred_element_type=F32
        )
        state["squares"] = state["squares"] + jnp.sum(
            chunk[:, width : width + 3].astype(F32), axis=1, keepdims=True
        )

    ring_visit(own_rows, front)
    scale = lax.rsqrt(state["squares"] / model + EPSILON)
    gate_value = scale * state["gate"]
    up_value = scale * state["up"]
    squashed = jax.nn.sigmoid(GLU_ALPHA * gate_value)
    glu_value = gate_value * squashed
    hidden = (gates * ((up_value + 1.0) * glu_value)).astype(BF16)

    def out_part(distance, half):
        rows = slots // 2
        left = hidden if half is None else hidden[half * rows : (half + 1) * rows]
        return jnp.dot(left, pick(down_stack, distance), preferred_element_type=F32)

    returned = over_seq(ring_sum(out_part).astype(BF16))
    moe_out = jnp.dot(taken, returned, preferred_element_type=F32)
    target = STEER * control / jnp.sqrt(jnp.sum(control * control))
    own_target = lax.dynamic_slice_in_dim(target, me * width, width, 0)
    residual_error = (mixed + moe_out - own_target[None, :]).astype(BF16)

    back = {"hidden": jnp.zeros((slots, hid), F32)}

    def backward(distance, chunk):
        back["hidden"] = back["hidden"] + lax.dot_general(
            chunk,
            pick(down_stack, distance),
            (((1,), (1,)), ((), ())),
            preferred_element_type=F32,
        )

    ring_visit(over_seq(to_slots(residual_error)), backward)
    d_hidden = (gates * scale) * back["hidden"]
    d_gate = (
        d_hidden
        * (up_value + 1.0)
        * (squashed + GLU_ALPHA * gate_value * squashed * (1.0 - squashed))
    ).astype(BF16)
    d_up = (d_hidden * glu_value).astype(BF16)

    both = jnp.concatenate([d_gate.T, d_up.T], axis=0)
    grads = lax.dot_general(
        both, state["rows"], (((1,), (1,)), ((), ())), preferred_element_type=F32
    ).astype(BF16)
    return grads.reshape(1, 2, hid, model).transpose(0, 1, 3, 2)


def solution(mesh):
    return jax.shard_map(
        shards,
        mesh=mesh,
        in_specs=(
            P("seq", "exp"),
            P("seq", "exp"),
            P("seq", "exp"),
            P("exp"),
            P("exp", None),
            P("seq", "exp"),
            P(),
            P("seq"),
            P("seq", None),
            P("seq", None),
            P("seq", None, None, "exp"),
            P("seq", "exp", None),
            P(),
        ),
        out_specs=P("seq", None, None, "exp"),
        check_vma=False,
    )
```

```python
import jax
import jax.numpy as jnp
from jax import lax
from jax.experimental import pallas as pl
from jax.experimental.pallas import tpu as pltpu
from jax.sharding import PartitionSpec as P

HEAD_DIM = 64
WINDOW = 128
TOPK = 4
GLU_ALPHA = 1.702
STEER = 6.5
EPSILON = 1e-05
MASKED = -1e30
BF16 = jnp.bfloat16
F32 = jnp.float32
DIRECT = 128


def passed_along(block, axis, distance):
    devices = range(lax.axis_size(axis))
    route = [(i - distance, i) for i in devices if i - distance in devices]
    return lax.ppermute(block, axis, route)


def attend(queries, attn_keys, attn_values, sink_logits, doc_start):
    seg_len = queries.shape[0]
    heads_here = queries.shape[1] // HEAD_DIM
    kv_here = attn_keys.shape[1] // HEAD_DIM
    group_size = heads_here // kv_here
    both_rims = passed_along(jnp.stack([attn_keys, attn_values]), "seq", 1)
    keys_all = jnp.concatenate([both_rims[0], attn_keys], axis=0).reshape(
        WINDOW + seg_len, kv_here, HEAD_DIM
    )
    values_all = jnp.concatenate([both_rims[1], attn_values], axis=0).reshape(
        WINDOW + seg_len, kv_here, HEAD_DIM
    )
    offset = lax.axis_index("seq") * seg_len
    query_pos = offset + jnp.arange(seg_len, dtype=jnp.int32)
    key_pos = offset - WINDOW + jnp.arange(WINDOW + seg_len, dtype=jnp.int32)
    allowed = (
        (key_pos[None, :] <= query_pos[:, None])
        & (key_pos[None, :] > query_pos[:, None] - WINDOW)
        & (key_pos[None, :] >= doc_start[:, None])
    )
    grouped = queries.reshape(seg_len, kv_here, group_size, HEAD_DIM)
    scores = jnp.einsum(
        "qcgd,kcd->cgqk", grouped, keys_all, preferred_element_type=F32
    ) * HEAD_DIM ** (-0.5)
    masked_scores = jnp.where(allowed[None, None], scores, MASKED)
    sink_grid = sink_logits.reshape(kv_here, group_size, 1, 1)
    row_top = jnp.maximum(jnp.max(masked_scores, axis=-1, keepdims=True), sink_grid)
    expo_scores = jnp.where(allowed[None, None], jnp.exp(masked_scores - row_top), 0.0)
    denominator = jnp.sum(expo_scores, axis=-1, keepdims=True) + jnp.exp(sink_grid - row_top)
    attn_weights = (expo_scores / denominator).astype(BF16)
    mixed_heads = jnp.einsum(
        "cgqk,kcd->qcgd", attn_weights, values_all, preferred_element_type=F32
    )
    return mixed_heads.astype(BF16).reshape(seg_len, heads_here * HEAD_DIM)


def up_ring(block):
    n = lax.axis_size("exp")
    return lax.ppermute(block, "exp", [(i, (i + 1) % n) for i in range(n)])


def down_ring(block):
    n = lax.axis_size("exp")
    return lax.ppermute(block, "exp", [(i, (i - 1) % n) for i in range(n)])


def ring_sum(part_for):
    n = lax.axis_size("exp")
    far = n // 2
    ahead = up_ring(part_for(far, 0).astype(BF16)).astype(F32)
    behind = down_ring(part_for(far, 1).astype(BF16)).astype(F32)
    rows = ahead.shape[0]
    for distance in range(far - 1, 0, -1):
        if distance == far - 1:
            ahead = jnp.pad(ahead, ((0, rows), (0, 0)))
            behind = jnp.pad(behind, ((rows, 0), (0, 0)))
        ahead = up_ring((part_for(distance, None) + ahead).astype(BF16)).astype(F32)
        behind = down_ring((part_for(-distance, None) + behind).astype(BF16)).astype(F32)
    return part_for(0, None) + ahead + behind


def direct_sum(part_for):
    n = lax.axis_size("exp")
    total = part_for(0).astype(F32)
    for distance in range(1, n):
        route = [(i, (i + distance) % n) for i in range(n)]
        total = total + lax.ppermute(part_for(distance), "exp", route).astype(F32)
    return total


def direct_gather(own):
    n = lax.axis_size("exp")
    me = lax.axis_index("exp")
    stacked = jnp.zeros((n,) + own.shape, own.dtype)
    for distance in range(n):
        route = [(i, (i + distance) % n) for i in range(n)]
        block = own if distance == 0 else lax.ppermute(own, "exp", route)
        stacked = lax.dynamic_update_index_in_dim(
            stacked, block, lax.rem(me - distance + n, n), 0
        )
    return stacked


def split_kernel(n_exp, w_ref, direct_ref, ring_ref):
    width = w_ref.shape[1] // n_exp
    for z in range(n_exp):
        block = w_ref[:, z * width : (z + 1) * width]
        direct_ref[:, z * DIRECT : (z + 1) * DIRECT] = block[:, :DIRECT]
        ring_ref[z] = block[:, DIRECT:]


def split_columns(w, n_exp):
    rows, columns = w.shape
    ring = columns // n_exp - DIRECT
    return pl.pallas_call(
        lambda *refs: split_kernel(n_exp, *refs),
        out_shape=(
            jax.ShapeDtypeStruct((rows, n_exp * DIRECT), BF16),
            jax.ShapeDtypeStruct((n_exp, rows, ring), BF16),
        ),
        compiler_params=pltpu.CompilerParams(vmem_limit_bytes=48 << 20),
        cost_estimate=pl.CostEstimate(
            flops=0, bytes_accessed=5 * rows * columns, transcendentals=0
        ),
        name="split_columns",
    )(w)


def grad_kernel(pairs, d_ref, direct_ref, ring_ref, out_ref):
    step = pl.program_id(0)
    d_value = d_ref[...]
    from_direct = jnp.dot(d_value, direct_ref[...], preferred_element_type=F32).astype(BF16)
    ring = ring_ref.shape[1]
    width = DIRECT + ring
    from_ring = [
        lax.dot_general(
            d_value, ring_ref[i], (((1,), (1,)), ((), ())), preferred_element_type=F32
        ).astype(BF16)
        for i in range(2)
    ]
    for pair in range(pairs):

        @pl.when(step == pair)
        def _():
            for i in range(2):
                first = (2 * pair + i) * width
                out_ref[:, first : first + DIRECT] = from_direct[
                    :, i * DIRECT : (i + 1) * DIRECT
                ]
                out_ref[:, first + DIRECT : first + width] = from_ring[i]


def grad_rows(d_value, direct_rows, ring_rows):
    n_exp, ring, slots = ring_rows.shape
    rows = d_value.shape[0]
    pairs = n_exp // 2
    return pl.pallas_call(
        lambda *refs: grad_kernel(pairs, *refs),
        out_shape=jax.ShapeDtypeStruct((rows, n_exp * (DIRECT + ring)), BF16),
        grid=(pairs,),
        in_specs=[
            pl.BlockSpec((rows, slots), lambda i: (0, 0)),
            pl.BlockSpec((slots, 2 * DIRECT), lambda i: (0, i)),
            pl.BlockSpec((2, ring, slots), lambda i: (i, 0, 0)),
        ],
        out_specs=pl.BlockSpec((rows, n_exp * (DIRECT + ring)), lambda i: (0, 0)),
        compiler_params=pltpu.CompilerParams(vmem_limit_bytes=48 << 20),
        name="grad_rows",
    )(d_value, direct_rows, ring_rows)


def ring_visit(own, visit):
    n = lax.axis_size("exp")
    far = n // 2
    ahead = behind = own
    visit(0, own)
    for distance in range(1, far):
        ahead = up_ring(ahead)
        behind = down_ring(behind)
        visit(-distance, ahead)
        visit(distance, behind)
    rows = own.shape[0] // 2
    ahead = up_ring(ahead[:rows])
    behind = down_ring(behind[rows:])
    visit(far, jnp.concatenate([ahead, behind], axis=0))


def over_seq(rows):
    n_seq = lax.axis_size("seq")
    blocks = rows.reshape(n_seq, rows.shape[0] // n_seq, rows.shape[1])
    return lax.all_to_all(blocks, "seq", split_axis=0, concat_axis=0, tiled=True).reshape(
        rows.shape
    )


def in_pieces(column):
    first = column.astype(BF16)
    second = (column - first.astype(F32)).astype(BF16)
    third = (column - first.astype(F32) - second.astype(F32)).astype(BF16)
    return [first, second, third]


def shards(
    queries,
    attn_keys,
    attn_values,
    sink_logits,
    out_proj,
    residual,
    norm_gain,
    doc_start,
    expert_ids,
    route_scores,
    w_gate_up,
    w_down,
    control,
):
    n_seq = lax.axis_size("seq")
    n_exp = lax.axis_size("exp")
    seg_len, width = residual.shape
    model = out_proj.shape[1]
    hid = w_down.shape[1]
    capacity = 2 * TOPK * seg_len // n_seq
    slots = n_seq * capacity
    me = lax.axis_index("exp")

    def chunk_at(distance):
        return lax.rem(me + distance + n_exp, n_exp)

    def pick(stacked, distance):
        return lax.dynamic_index_in_dim(stacked, chunk_at(distance), 0, keepdims=False)

    heads_out = attend(queries, attn_keys, attn_values, sink_logits, doc_start)
    partial_value = jnp.dot(heads_out, out_proj, preferred_element_type=F32).astype(BF16)
    partial_chunks = partial_value.reshape(seg_len, n_exp, width).transpose(1, 0, 2)

    mixed = direct_sum(lambda distance: pick(partial_chunks, distance)) + residual.astype(F32)

    experts = jnp.arange(n_seq, dtype=jnp.int32)
    named = expert_ids[:, :, None] == experts[None, None, :]
    member = jnp.any(named, axis=1)
    route_gates = route_scores / jnp.sum(route_scores, axis=-1, keepdims=True)
    gate_table = jnp.sum(jnp.where(named, route_gates[:, :, None], 0.0), axis=1)
    position = jnp.arange(seg_len, dtype=jnp.int32)
    earlier = (position[:, None] > position[None, :]).astype(BF16)
    rank = jnp.dot(earlier, member.astype(BF16), preferred_element_type=F32)
    place = jnp.where(member, rank + 1.0, 0.0).astype(BF16)
    slot = jnp.arange(slots, dtype=jnp.int32)
    spread = (slot[None, :] // capacity == experts[:, None]).astype(BF16)
    place_wide = jnp.dot(place, spread, preferred_element_type=F32)
    taken = (place_wide == (slot % capacity + 1).astype(F32)[None, :]).astype(BF16)
    gate_wide = jnp.dot(gate_table, spread.astype(F32), precision=lax.Precision.HIGHEST)
    gate_slot = jnp.sum(taken.astype(F32) * gate_wide, axis=0)

    def to_slots(rows):
        return lax.dot_general(
            taken, rows, (((0,), (0,)), ((), ())), preferred_element_type=F32
        ).astype(BF16)

    def to_experts(own, extras, visit):
        sent = to_slots(own[:, DIRECT:])
        if extras:
            sent = jnp.concatenate([sent] + extras, axis=1)
        ring_rows = over_seq(sent)
        gathered = direct_gather(own[:, :DIRECT])
        sent = to_slots(gathered.transpose(1, 0, 2).reshape(seg_len, n_exp * DIRECT))
        direct_rows = over_seq(sent)
        ring_visit(ring_rows, visit)
        return ring_rows, direct_rows

    ring = width - DIRECT
    gain = lax.dynamic_slice_in_dim(norm_gain, me * width, width, 0)
    squares = jnp.sum(mixed * mixed, axis=1, keepdims=True)
    slot_squares = to_slots(jnp.concatenate(in_pieces(squares), axis=1))
    extras = [slot_squares] + in_pieces(gate_slot[:, None])

    up_direct, up_ring_stack = split_columns(
        w_gate_up[0].transpose(0, 2, 1).reshape(2 * hid, model), n_exp
    )
    down_direct, down_ring_stack = split_columns(w_down[0], n_exp)

    state = {
        "rows": jnp.zeros((n_exp, ring, slots), BF16),
        "value": jnp.zeros((2 * hid, slots), F32),
        "squares": jnp.zeros((slots,), F32),
    }

    def front(distance, chunk):
        rows = chunk[:, :ring].T
        state["rows"] = lax.dynamic_update_index_in_dim(
            state["rows"], rows, chunk_at(distance), 0
        )
        state["value"] = state["value"] + jnp.dot(
            pick(up_ring_stack, distance), rows, preferred_element_type=F32
        )
        state["squares"] = state["squares"] + jnp.sum(
            chunk[:, ring : ring + 3].astype(F32), axis=1
        )

    own_rows, direct_rows = to_experts((mixed * gain[None, :]).astype(BF16), extras, front)
    gates = jnp.sum(own_rows[:, ring + 3 : ring + 6].astype(F32), axis=1)[None, :]
    value = state["value"] + lax.dot_general(
        up_direct, direct_rows, (((1,), (1,)), ((), ())), preferred_element_type=F32
    )
    scale = lax.rsqrt(state["squares"] / model + EPSILON)[None, :]
    gate_value = scale * value[:hid]
    up_value = scale * value[hid:]
    squashed = jax.nn.sigmoid(GLU_ALPHA * gate_value)
    glu_value = gate_value * squashed
    hidden = (gates * ((up_value + 1.0) * glu_value)).astype(BF16).T

    direct_out = jnp.dot(hidden, down_direct, preferred_element_type=F32).astype(BF16)
    direct_back = over_seq(direct_out)

    def out_part(distance, half):
        rows = slots // 2
        left = hidden if half is None else hidden[half * rows : (half + 1) * rows]
        return jnp.dot(left, pick(down_ring_stack, distance), preferred_element_type=F32)

    ring_back = over_seq(ring_sum(out_part).astype(BF16))
    direct_parts = (
        jnp.dot(taken, direct_back, preferred_element_type=F32)
        .astype(BF16)
        .reshape(seg_len, n_exp, DIRECT)
        .transpose(1, 0, 2)
    )
    moe_out = jnp.concatenate(
        [
            direct_sum(lambda distance: pick(direct_parts, distance)),
            jnp.dot(taken, ring_back, preferred_element_type=F32),
        ],
        axis=1,
    )
    target = STEER * control / jnp.sqrt(jnp.sum(control * control))
    own_target = lax.dynamic_slice_in_dim(target, me * width, width, 0)
    residual_error = (mixed + moe_out - own_target[None, :]).astype(BF16)

    back = {"hidden": jnp.zeros((hid, slots), F32)}

    def backward(distance, chunk):
        back["hidden"] = back["hidden"] + jnp.dot(
            pick(down_ring_stack, distance), chunk.T, preferred_element_type=F32
        )

    _, direct_error = to_experts(residual_error, [], backward)
    d_hidden = (gates * scale) * (
        back["hidden"]
        + lax.dot_general(
            down_direct, direct_error, (((1,), (1,)), ((), ())), preferred_element_type=F32
        )
    )
    d_gate = (
        d_hidden
        * (up_value + 1.0)
        * (squashed + GLU_ALPHA * gate_value * squashed * (1.0 - squashed))
    ).astype(BF16)
    d_up = (d_hidden * glu_value).astype(BF16)
    grads = grad_rows(jnp.concatenate([d_gate, d_up], axis=0), direct_rows, state["rows"])
    return grads.reshape(1, 2, hid, model).transpose(0, 1, 3, 2)


def solution(mesh):
    return jax.shard_map(
        shards,
        mesh=mesh,
        in_specs=(
            P("seq", "exp"),
            P("seq", "exp"),
            P("seq", "exp"),
            P("exp"),
            P("exp", None),
            P("seq", "exp"),
            P(),
            P("seq"),
            P("seq", None),
            P("seq", None),
            P("seq", None, None, "exp"),
            P("seq", "exp", None),
            P(),
        ),
        out_specs=P("seq", None, None, "exp"),
        check_vma=False,
    )
```

```python
import jax
import jax.numpy as jnp
from jax import lax
from jax.experimental import pallas as pl
from jax.experimental.layout import Layout, with_layout_constraint
from jax.experimental.pallas import tpu as pltpu
from jax.sharding import PartitionSpec as P

HEAD_DIM = 64
WINDOW = 128
TOPK = 4
GLU_ALPHA = 1.702
STEER = 6.5
EPSILON = 1e-05
MASKED = -1e30
BF16 = jnp.bfloat16
F32 = jnp.float32
PIECE = 192


def passed_along(block, axis, distance):
    devices = range(lax.axis_size(axis))
    route = [(i - distance, i) for i in devices if i - distance in devices]
    return lax.ppermute(block, axis, route)


def attend(queries, attn_keys, attn_values, sink_logits, doc_start):
    seg_len = queries.shape[0]
    heads_here = queries.shape[1] // HEAD_DIM
    kv_here = attn_keys.shape[1] // HEAD_DIM
    group_size = heads_here // kv_here
    both_rims = passed_along(jnp.stack([attn_keys, attn_values]), "seq", 1)
    keys_all = jnp.concatenate([both_rims[0], attn_keys], axis=0).reshape(
        WINDOW + seg_len, kv_here, HEAD_DIM
    )
    values_all = jnp.concatenate([both_rims[1], attn_values], axis=0).reshape(
        WINDOW + seg_len, kv_here, HEAD_DIM
    )
    offset = lax.axis_index("seq") * seg_len
    query_pos = offset + jnp.arange(seg_len, dtype=jnp.int32)
    key_pos = offset - WINDOW + jnp.arange(WINDOW + seg_len, dtype=jnp.int32)
    allowed = (
        (key_pos[None, :] <= query_pos[:, None])
        & (key_pos[None, :] > query_pos[:, None] - WINDOW)
        & (key_pos[None, :] >= doc_start[:, None])
    )
    grouped = queries.reshape(seg_len, kv_here, group_size, HEAD_DIM)
    scores = jnp.einsum(
        "qcgd,kcd->cgqk", grouped, keys_all, preferred_element_type=F32
    ) * HEAD_DIM ** (-0.5)
    masked_scores = jnp.where(allowed[None, None], scores, MASKED)
    sink_grid = sink_logits.reshape(kv_here, group_size, 1, 1)
    row_top = jnp.maximum(jnp.max(masked_scores, axis=-1, keepdims=True), sink_grid)
    expo_scores = jnp.where(allowed[None, None], jnp.exp(masked_scores - row_top), 0.0)
    denominator = jnp.sum(expo_scores, axis=-1, keepdims=True) + jnp.exp(sink_grid - row_top)
    attn_weights = (expo_scores / denominator).astype(BF16)
    mixed_heads = jnp.einsum(
        "cgqk,kcd->qcgd", attn_weights, values_all, preferred_element_type=F32
    )
    return mixed_heads.astype(BF16).reshape(seg_len, heads_here * HEAD_DIM)


def up_ring(block):
    n = lax.axis_size("exp")
    return lax.ppermute(block, "exp", [(i, (i + 1) % n) for i in range(n)])


def down_ring(block):
    n = lax.axis_size("exp")
    return lax.ppermute(block, "exp", [(i, (i - 1) % n) for i in range(n)])


def ring_sum(part_for, far_ahead, hold=None):
    far = lax.axis_size("exp") // 2
    sums = []
    for move, sign, steps in (
        (up_ring, 1, far if far_ahead else far - 1),
        (down_ring, -1, far - 1 if far_ahead else far),
    ):
        total = None
        for distance in range(steps, 0, -1):
            share = part_for(sign * distance)
            total = share if total is None else share + total
            moved = move(total.astype(BF16))
            if distance == 2 and steps == far and hold is not None:
                moved, hold = lax.optimization_barrier((moved, hold))
            total = moved.astype(F32)
        sums.append(total)
    return part_for(0) + sums[0] + sums[1], hold


def direct_sum(part_for):
    n = lax.axis_size("exp")
    total = part_for(0).astype(F32)
    for distance in range(1, n):
        route = [(i, (i + distance) % n) for i in range(n)]
        total = total + lax.ppermute(part_for(distance), "exp", route).astype(F32)
    return total


def split_kernel(n_exp, w_ref, first_ref, second_ref):
    width = w_ref.shape[1] // n_exp
    for z in range(n_exp):
        block = w_ref[:, z * width : (z + 1) * width]
        first_ref[z] = block[:, :PIECE]
        second_ref[z] = block[:, PIECE:]


def split_columns(w, n_exp):
    rows, columns = w.shape
    width = columns // n_exp
    return pl.pallas_call(
        lambda *refs: split_kernel(n_exp, *refs),
        out_shape=(
            jax.ShapeDtypeStruct((n_exp, rows, PIECE), BF16),
            jax.ShapeDtypeStruct((n_exp, rows, width - PIECE), BF16),
        ),
        compiler_params=pltpu.CompilerParams(vmem_limit_bytes=48 << 20),
        cost_estimate=pl.CostEstimate(
            flops=0, bytes_accessed=5 * rows * columns, transcendentals=0
        ),
        name="split_columns",
    )(w)


def grad_kernel(d_ref, rows_ref, out_ref):
    n_exp, width, _ = rows_ref.shape
    for z in range(n_exp):
        out_ref[:, z * width : (z + 1) * width] = lax.dot_general(
            d_ref[...], rows_ref[z], (((1,), (1,)), ((), ())), preferred_element_type=F32
        ).astype(BF16)


def grad_rows(d_value, rows):
    n_exp, width, slots = rows.shape
    hid = d_value.shape[1]
    return pl.pallas_call(
        grad_kernel,
        out_shape=jax.ShapeDtypeStruct((2, hid, n_exp * width), BF16),
        grid=(2,),
        in_specs=[
            pl.BlockSpec((None, hid, slots), lambda i: (i, 0, 0)),
            pl.BlockSpec((n_exp, width, slots), lambda i: (0, 0, 0)),
        ],
        out_specs=pl.BlockSpec((None, hid, n_exp * width), lambda i: (i, 0, 0)),
        compiler_params=pltpu.CompilerParams(vmem_limit_bytes=48 << 20),
        name="grad_rows",
    )(d_value, rows)


def ring_visit(own, visit, far_ahead, hold=None):
    far = lax.axis_size("exp") // 2
    own = with_layout_constraint(own, Layout((1, 0)))
    ahead = behind = own
    visit(0, own)
    for distance in range(1, far + 1):
        if distance < far or far_ahead:
            ahead = up_ring(ahead)
        if distance < far or not far_ahead:
            behind = down_ring(behind)
        if distance == 1 and hold is not None:
            ahead, hold = lax.optimization_barrier((ahead, hold))
        if distance < far:
            visit(-distance, ahead)
            visit(distance, behind)
    visit(far, ahead if far_ahead else behind)
    return hold


def over_seq(rows):
    n_seq = lax.axis_size("seq")
    blocks = rows.reshape(n_seq, rows.shape[0] // n_seq, rows.shape[1])
    return lax.all_to_all(blocks, "seq", split_axis=0, concat_axis=0, tiled=True).reshape(
        rows.shape
    )


def in_pieces(column):
    first = column.astype(BF16)
    second = (column - first.astype(F32)).astype(BF16)
    third = (column - first.astype(F32) - second.astype(F32)).astype(BF16)
    return [first, second, third]


def shards(
    queries,
    attn_keys,
    attn_values,
    sink_logits,
    out_proj,
    residual,
    norm_gain,
    doc_start,
    expert_ids,
    route_scores,
    w_gate_up,
    w_down,
    control,
):
    n_seq = lax.axis_size("seq")
    n_exp = lax.axis_size("exp")
    seg_len, width = residual.shape
    model = out_proj.shape[1]
    hid = w_down.shape[1]
    capacity = 2 * TOPK * seg_len // n_seq
    slots = n_seq * capacity
    me = lax.axis_index("exp")

    def chunk_at(distance):
        return lax.rem(me + distance + n_exp, n_exp)

    def pick(stacked, distance):
        return lax.dynamic_index_in_dim(stacked, chunk_at(distance), 0, keepdims=False)

    heads_out = attend(queries, attn_keys, attn_values, sink_logits, doc_start)
    partial_value = jnp.dot(heads_out, out_proj, preferred_element_type=F32).astype(BF16)
    partial_chunks = partial_value.reshape(seg_len, n_exp, width).transpose(1, 0, 2)

    mixed = direct_sum(lambda distance: pick(partial_chunks, distance)) + residual.astype(F32)

    experts = jnp.arange(n_seq, dtype=jnp.int32)
    named = expert_ids[:, :, None] == experts[None, None, :]
    member = jnp.any(named, axis=1)
    route_gates = route_scores / jnp.sum(route_scores, axis=-1, keepdims=True)
    gate_table = jnp.sum(jnp.where(named, route_gates[:, :, None], 0.0), axis=1)
    position = jnp.arange(seg_len, dtype=jnp.int32)
    earlier = (position[:, None] > position[None, :]).astype(BF16)
    rank = jnp.dot(earlier, member.astype(BF16), preferred_element_type=F32)
    place = jnp.where(member, rank + 1.0, 0.0).astype(BF16)
    slot = jnp.arange(slots, dtype=jnp.int32)
    spread = (slot[None, :] // capacity == experts[:, None]).astype(BF16)
    place_wide = jnp.dot(place, spread, preferred_element_type=F32)
    taken = (place_wide == (slot % capacity + 1).astype(F32)[None, :]).astype(BF16)
    gate_wide = jnp.dot(gate_table, spread.astype(F32), precision=lax.Precision.HIGHEST)
    gate_slot = jnp.sum(taken.astype(F32) * gate_wide, axis=0)

    def to_slots(rows):
        return lax.dot_general(
            taken, rows, (((0,), (0,)), ((), ())), preferred_element_type=F32
        ).astype(BF16)

    gain = lax.dynamic_slice_in_dim(norm_gain, me * width, width, 0)
    squares = jnp.sum(mixed * mixed, axis=1, keepdims=True)
    scaled = (mixed * gain[None, :]).astype(BF16)
    sent = [
        jnp.concatenate(
            [to_slots(jnp.concatenate([scaled[:, :PIECE]] + in_pieces(squares), axis=1))]
            + in_pieces(gate_slot[:, None]),
            axis=1,
        ),
        to_slots(scaled[:, PIECE:]),
    ]
    firsts = (0, PIECE)
    ends = (PIECE, width)

    up_weights = w_gate_up[0].transpose(0, 2, 1).reshape(2 * hid, model)
    up_weights, down_weights, sent[0] = lax.optimization_barrier(
        (up_weights, w_down[0], sent[0])
    )
    up_stacks = split_columns(up_weights, n_exp)
    down_stacks = split_columns(down_weights, n_exp)

    state = {
        "rows": jnp.zeros((n_exp, width, slots), BF16),
        "value": jnp.zeros((2 * hid, slots), F32),
        "squares": jnp.zeros((slots,), F32),
    }

    def front(piece):
        def visit(distance, chunk):
            size = ends[piece] - firsts[piece]
            rows = chunk[:, :size].T
            state["rows"] = lax.dynamic_update_slice(
                state["rows"], rows[None], (chunk_at(distance), firsts[piece], 0)
            )
            state["value"] = state["value"] + jnp.dot(
                pick(up_stacks[piece], distance), rows, preferred_element_type=F32
            )
            if piece == 0:
                state["squares"] = state["squares"] + jnp.sum(
                    chunk[:, size : size + 3].astype(F32), axis=1
                )

        return visit

    own_rows = over_seq(sent[0])
    gates = jnp.sum(own_rows[:, PIECE + 3 : PIECE + 6].astype(F32), axis=1)[None, :]
    sent[1] = ring_visit(own_rows, front(0), True, sent[1])
    ring_visit(over_seq(sent[1]), front(1), False)
    scale = lax.rsqrt(state["squares"] / model + EPSILON)[None, :]
    gate_value = scale * state["value"][:hid]
    up_value = scale * state["value"][hid:]
    squashed = jax.nn.sigmoid(GLU_ALPHA * gate_value)
    glu_value = gate_value * squashed
    hidden = (gates * ((up_value + 1.0) * glu_value)).astype(BF16).T

    target = STEER * control / jnp.sqrt(jnp.sum(control * control))
    own_target = lax.dynamic_slice_in_dim(target, me * width, width, 0)
    back = {"hidden": jnp.zeros((hid, slots), F32)}

    def out_part(piece, left):
        return lambda distance: jnp.dot(
            left, pick(down_stacks[piece], distance), preferred_element_type=F32
        )

    def error_rows(piece, total):
        columns = slice(firsts[piece], ends[piece])
        moe_out = jnp.dot(taken, over_seq(total.astype(BF16)), preferred_element_type=F32)
        error = mixed[:, columns] + moe_out - own_target[None, columns]
        return over_seq(to_slots(error.astype(BF16)))

    def backward(piece):
        def visit(distance, chunk):
            back["hidden"] = back["hidden"] + jnp.dot(
                pick(down_stacks[piece], distance), chunk.T, preferred_element_type=F32
            )

        return visit

    total, left = ring_sum(out_part(0, hidden), True, hidden)
    second, _ = ring_sum(out_part(1, left), False)
    ring_visit(error_rows(0, total), backward(0), True)
    ring_visit(error_rows(1, second), backward(1), False)
    d_hidden = (gates * scale) * back["hidden"]
    d_gate = (
        d_hidden
        * (up_value + 1.0)
        * (squashed + GLU_ALPHA * gate_value * squashed * (1.0 - squashed))
    ).astype(BF16)
    d_up = (d_hidden * glu_value).astype(BF16)
    grads = grad_rows(jnp.stack([d_gate, d_up]), state["rows"])
    return grads[None].transpose(0, 1, 3, 2)


def solution(mesh):
    return jax.shard_map(
        shards,
        mesh=mesh,
        in_specs=(
            P("seq", "exp"),
            P("seq", "exp"),
            P("seq", "exp"),
            P("exp"),
            P("exp", None),
            P("seq", "exp"),
            P(),
            P("seq"),
            P("seq", None),
            P("seq", None),
            P("seq", None, None, "exp"),
            P("seq", "exp", None),
            P(),
        ),
        out_specs=P("seq", None, None, "exp"),
        check_vma=False,
    )
```

```python
import jax
import jax.numpy as jnp
from jax import lax
from jax.experimental import pallas as pl
from jax.experimental.layout import Layout, with_layout_constraint
from jax.experimental.pallas import tpu as pltpu
from jax.sharding import PartitionSpec as P

HEAD_DIM = 64
WINDOW = 128
TOPK = 4
GLU_ALPHA = 1.702
STEER = 6.5
EPSILON = 1e-05
MASKED = -1e30
BF16 = jnp.bfloat16
F32 = jnp.float32
GRAD_BLOCK = 768


def passed_along(block, axis, distance):
    devices = range(lax.axis_size(axis))
    route = [(i - distance, i) for i in devices if i - distance in devices]
    return lax.ppermute(block, axis, route)


def attend(queries, attn_keys, attn_values, sink_logits, doc_start):
    seg_len = queries.shape[0]
    heads_here = queries.shape[1] // HEAD_DIM
    kv_here = attn_keys.shape[1] // HEAD_DIM
    group_size = heads_here // kv_here
    both_rims = passed_along(jnp.stack([attn_keys, attn_values]), "seq", 1)
    keys_all = jnp.concatenate([both_rims[0], attn_keys], axis=0).reshape(
        WINDOW + seg_len, kv_here, HEAD_DIM
    )
    values_all = jnp.concatenate([both_rims[1], attn_values], axis=0).reshape(
        WINDOW + seg_len, kv_here, HEAD_DIM
    )
    offset = lax.axis_index("seq") * seg_len
    query_pos = offset + jnp.arange(seg_len, dtype=jnp.int32)
    key_pos = offset - WINDOW + jnp.arange(WINDOW + seg_len, dtype=jnp.int32)
    allowed = (
        (key_pos[None, :] <= query_pos[:, None])
        & (key_pos[None, :] > query_pos[:, None] - WINDOW)
        & (key_pos[None, :] >= doc_start[:, None])
    )
    grouped = queries.reshape(seg_len, kv_here, group_size, HEAD_DIM)
    scores = jnp.einsum(
        "qcgd,kcd->cgqk", grouped, keys_all, preferred_element_type=F32
    ) * HEAD_DIM ** (-0.5)
    masked_scores = jnp.where(allowed[None, None], scores, MASKED)
    sink_grid = sink_logits.reshape(kv_here, group_size, 1, 1)
    row_top = jnp.maximum(jnp.max(masked_scores, axis=-1, keepdims=True), sink_grid)
    expo_scores = jnp.where(allowed[None, None], jnp.exp(masked_scores - row_top), 0.0)
    denominator = jnp.sum(expo_scores, axis=-1, keepdims=True) + jnp.exp(sink_grid - row_top)
    attn_weights = (expo_scores / denominator).astype(BF16)
    mixed_heads = jnp.einsum(
        "cgqk,kcd->qcgd", attn_weights, values_all, preferred_element_type=F32
    )
    return mixed_heads.astype(BF16).reshape(seg_len, heads_here * HEAD_DIM)


def up_ring(block):
    n = lax.axis_size("exp")
    return lax.ppermute(block, "exp", [(i, (i + 1) % n) for i in range(n)])


def down_ring(block):
    n = lax.axis_size("exp")
    return lax.ppermute(block, "exp", [(i, (i - 1) % n) for i in range(n)])


def ring_sum(part_for):
    far = lax.axis_size("exp") // 2
    ahead = up_ring(part_for(far, 0).astype(BF16)).astype(F32)
    behind = down_ring(part_for(far, 1).astype(BF16)).astype(F32)
    rows = ahead.shape[0]
    ahead = jnp.pad(ahead, ((0, rows), (0, 0)))
    behind = jnp.pad(behind, ((rows, 0), (0, 0)))
    for distance in range(far - 1, 0, -1):
        ahead = up_ring((part_for(distance, None) + ahead).astype(BF16)).astype(F32)
        behind = down_ring((part_for(-distance, None) + behind).astype(BF16)).astype(F32)
    return part_for(0, None) + ahead + behind


def ring_visit(own, visit):
    far = lax.axis_size("exp") // 2
    own = with_layout_constraint(own, Layout((1, 0)))
    ahead = behind = own
    for distance in range(1, far):
        ahead = up_ring(ahead)
        behind = down_ring(behind)
        visit(1 - distance, own if distance == 1 else last[0])
        if distance > 1:
            visit(distance - 1, last[1])
        last = (ahead, behind)
    rows = own.shape[0] // 2
    ahead = up_ring(ahead[:rows])
    behind = down_ring(behind[rows:])
    visit(1 - far, last[0])
    visit(far - 1, last[1])
    visit(far, jnp.concatenate([ahead, behind], axis=0))


def two_stage_sum(chunks):
    n = lax.axis_size("exp")
    me = lax.axis_index("exp")
    pairs, odd = me // 2, lax.rem(me, 2)
    paired = chunks.reshape((n // 2, 2) + chunks.shape[1:])
    mine = lax.dynamic_index_in_dim(paired, odd, 1, keepdims=False)
    others = lax.dynamic_index_in_dim(paired, 1 - odd, 1, keepdims=False)
    swapped = lax.ppermute(others, "exp", [(i, i ^ 1) for i in range(n)])
    sums = mine.astype(F32) + swapped.astype(F32)
    total = lax.dynamic_index_in_dim(sums, pairs, 0, keepdims=False)
    sums = sums.astype(BF16)
    for distance in range(1, n // 2):
        share = lax.dynamic_index_in_dim(
            sums, lax.rem(pairs + distance, n // 2), 0, keepdims=False
        )
        route = [(i, (i + 2 * distance) % n) for i in range(n)]
        total = total + lax.ppermute(share, "exp", route).astype(F32)
    return total


def split_kernel(n_exp, w_ref, out_ref):
    width = w_ref.shape[1] // n_exp
    for z in range(n_exp):
        out_ref[z] = w_ref[:, z * width : (z + 1) * width]


def split_columns(w, n_exp):
    rows, columns = w.shape
    return pl.pallas_call(
        lambda *refs: split_kernel(n_exp, *refs),
        out_shape=jax.ShapeDtypeStruct((n_exp, rows, columns // n_exp), BF16),
        compiler_params=pltpu.CompilerParams(vmem_limit_bytes=48 << 20),
        cost_estimate=pl.CostEstimate(
            flops=0, bytes_accessed=5 * rows * columns, transcendentals=0
        ),
        name="split_columns",
    )(w)


def grad_kernel(d_ref, rows_ref, out_ref):
    out_ref[...] = lax.dot_general(
        d_ref[...], rows_ref[...], (((1,), (1,)), ((), ())), preferred_element_type=F32
    ).astype(BF16)


def grad_rows(d_value, rows):
    count, slots = d_value.shape
    model = rows.shape[0]
    block = min(GRAD_BLOCK, model)
    return pl.pallas_call(
        grad_kernel,
        out_shape=jax.ShapeDtypeStruct((count, model), BF16),
        grid=(pl.cdiv(model, block),),
        in_specs=[
            pl.BlockSpec((count, slots), lambda i: (0, 0)),
            pl.BlockSpec((block, slots), lambda i: (i, 0)),
        ],
        out_specs=pl.BlockSpec((count, block), lambda i: (0, i)),
        compiler_params=pltpu.CompilerParams(vmem_limit_bytes=48 << 20),
        name="grad_rows",
    )(d_value, rows)


def over_seq(rows):
    n_seq = lax.axis_size("seq")
    blocks = rows.reshape(n_seq, rows.shape[0] // n_seq, rows.shape[1])
    return lax.all_to_all(blocks, "seq", split_axis=0, concat_axis=0, tiled=True).reshape(
        rows.shape
    )


def in_pieces(column):
    first = column.astype(BF16)
    second = (column - first.astype(F32)).astype(BF16)
    third = (column - first.astype(F32) - second.astype(F32)).astype(BF16)
    return [first, second, third]


def shards(
    queries,
    attn_keys,
    attn_values,
    sink_logits,
    out_proj,
    residual,
    norm_gain,
    doc_start,
    expert_ids,
    route_scores,
    w_gate_up,
    w_down,
    control,
):
    n_seq = lax.axis_size("seq")
    n_exp = lax.axis_size("exp")
    seg_len, width = residual.shape
    model = out_proj.shape[1]
    hid = w_down.shape[1]
    capacity = 2 * TOPK * seg_len // n_seq
    slots = n_seq * capacity
    me = lax.axis_index("exp")

    def chunk_at(distance):
        return lax.rem(me + distance + n_exp, n_exp)

    def pick(stacked, distance):
        return lax.dynamic_index_in_dim(stacked, chunk_at(distance), 0, keepdims=False)

    heads_out = attend(queries, attn_keys, attn_values, sink_logits, doc_start)
    partial_value = jnp.dot(heads_out, out_proj, preferred_element_type=F32).astype(BF16)
    partial_chunks = partial_value.reshape(seg_len, n_exp, width).transpose(1, 0, 2)

    mixed = two_stage_sum(partial_chunks) + residual.astype(F32)

    experts = jnp.arange(n_seq, dtype=jnp.int32)
    named = expert_ids[:, :, None] == experts[None, None, :]
    member = jnp.any(named, axis=1)
    route_gates = route_scores / jnp.sum(route_scores, axis=-1, keepdims=True)
    gate_table = jnp.sum(jnp.where(named, route_gates[:, :, None], 0.0), axis=1)
    position = jnp.arange(seg_len, dtype=jnp.int32)
    earlier = (position[:, None] > position[None, :]).astype(BF16)
    rank = jnp.dot(earlier, member.astype(BF16), preferred_element_type=F32)
    place = jnp.where(member, rank + 1.0, 0.0).astype(BF16)
    slot = jnp.arange(slots, dtype=jnp.int32)
    spread = (slot[None, :] // capacity == experts[:, None]).astype(BF16)
    place_wide = jnp.dot(place, spread, preferred_element_type=F32)
    taken = (place_wide == (slot % capacity + 1).astype(F32)[None, :]).astype(BF16)
    gate_wide = jnp.dot(gate_table, spread.astype(F32), precision=lax.Precision.HIGHEST)
    gate_slot = jnp.sum(taken.astype(F32) * gate_wide, axis=0)

    def to_slots(rows):
        return lax.dot_general(
            taken, rows, (((0,), (0,)), ((), ())), preferred_element_type=F32
        ).astype(BF16)

    gain = lax.dynamic_slice_in_dim(norm_gain, me * width, width, 0)
    squares = jnp.sum(mixed * mixed, axis=1, keepdims=True)
    scaled = (mixed * gain[None, :]).astype(BF16)
    sent = jnp.concatenate(
        [to_slots(jnp.concatenate([scaled] + in_pieces(squares), axis=1))]
        + in_pieces(gate_slot[:, None]),
        axis=1,
    )
    down, sent = lax.optimization_barrier((w_down[0], sent))
    down_stack = split_columns(down, n_exp)

    def all_rows(own, visit=None):
        box = [jnp.zeros((n_exp, width, slots), BF16)]

        def store(distance, chunk):
            box[0] = lax.dynamic_update_index_in_dim(
                box[0], chunk[:, :width].T, chunk_at(distance), 0
            )
            if visit is not None:
                visit(chunk)

        ring_visit(own, store)
        return box[0].reshape(model, slots)

    square_sums = []
    own_rows = over_seq(sent)
    gates = jnp.sum(own_rows[:, width + 3 : width + 6].astype(F32), axis=1)[None, :]
    rows = all_rows(
        own_rows,
        lambda chunk: square_sums.append(
            jnp.sum(chunk[:, width : width + 3].astype(F32), axis=1)
        ),
    )
    scale = lax.rsqrt(sum(square_sums) / model + EPSILON)[None, :]
    up_weights = w_gate_up[0].transpose(0, 2, 1).reshape(2 * hid, model)
    value = scale * jnp.dot(up_weights, rows, preferred_element_type=F32)
    gate_value = value[:hid]
    up_value = value[hid:]
    squashed = jax.nn.sigmoid(GLU_ALPHA * gate_value)
    glu_value = gate_value * squashed
    hidden = (gates * ((up_value + 1.0) * glu_value)).astype(BF16).T

    def out_part(distance, half):
        count = slots // 2
        left = hidden if half is None else hidden[half * count : (half + 1) * count]
        return jnp.dot(left, pick(down_stack, distance), preferred_element_type=F32)

    returned = over_seq(ring_sum(out_part).astype(BF16))
    moe_out = jnp.dot(taken, returned, preferred_element_type=F32)
    target = STEER * control / jnp.sqrt(jnp.sum(control * control))
    own_target = lax.dynamic_slice_in_dim(target, me * width, width, 0)
    residual_error = (mixed + moe_out - own_target[None, :]).astype(BF16)

    error_rows = all_rows(over_seq(to_slots(residual_error)))
    d_hidden = (gates * scale) * jnp.dot(w_down[0], error_rows, preferred_element_type=F32)
    d_gate = (
        d_hidden
        * (up_value + 1.0)
        * (squashed + GLU_ALPHA * gate_value * squashed * (1.0 - squashed))
    ).astype(BF16)
    d_up = (d_hidden * glu_value).astype(BF16)
    grads = grad_rows(jnp.concatenate([d_gate, d_up], axis=0), rows)
    return grads.reshape(1, 2, hid, model).transpose(0, 1, 3, 2)


def solution(mesh):
    return jax.shard_map(
        shards,
        mesh=mesh,
        in_specs=(
            P("seq", "exp"),
            P("seq", "exp"),
            P("seq", "exp"),
            P("exp"),
            P("exp", None),
            P("seq", "exp"),
            P(),
            P("seq"),
            P("seq", None),
            P("seq", None),
            P("seq", None, None, "exp"),
            P("seq", "exp", None),
            P(),
        ),
        out_specs=P("seq", None, None, "exp"),
        check_vma=False,
    )
```

```python
import jax
import jax.numpy as jnp
from jax import lax
from jax.experimental import pallas as pl
from jax.experimental.layout import Layout, with_layout_constraint
from jax.experimental.pallas import tpu as pltpu
from jax.sharding import PartitionSpec as P

HEAD_DIM = 64
WINDOW = 128
TOPK = 4
GLU_ALPHA = 1.702
STEER = 6.5
EPSILON = 1e-05
MASKED = -1e30
BF16 = jnp.bfloat16
F32 = jnp.float32
DIRECT = 128


def passed_along(block, axis, distance):
    devices = range(lax.axis_size(axis))
    route = [(i - distance, i) for i in devices if i - distance in devices]
    return lax.ppermute(block, axis, route)


def attend(queries, attn_keys, attn_values, sink_logits, doc_start):
    seg_len = queries.shape[0]
    heads_here = queries.shape[1] // HEAD_DIM
    kv_here = attn_keys.shape[1] // HEAD_DIM
    group_size = heads_here // kv_here
    both_rims = passed_along(jnp.stack([attn_keys, attn_values]), "seq", 1)
    keys_all = jnp.concatenate([both_rims[0], attn_keys], axis=0).reshape(
        WINDOW + seg_len, kv_here, HEAD_DIM
    )
    values_all = jnp.concatenate([both_rims[1], attn_values], axis=0).reshape(
        WINDOW + seg_len, kv_here, HEAD_DIM
    )
    offset = lax.axis_index("seq") * seg_len
    query_pos = offset + jnp.arange(seg_len, dtype=jnp.int32)
    key_pos = offset - WINDOW + jnp.arange(WINDOW + seg_len, dtype=jnp.int32)
    allowed = (
        (key_pos[None, :] <= query_pos[:, None])
        & (key_pos[None, :] > query_pos[:, None] - WINDOW)
        & (key_pos[None, :] >= doc_start[:, None])
    )
    grouped = queries.reshape(seg_len, kv_here, group_size, HEAD_DIM)
    scores = jnp.einsum(
        "qcgd,kcd->cgqk", grouped, keys_all, preferred_element_type=F32
    ) * HEAD_DIM ** (-0.5)
    masked_scores = jnp.where(allowed[None, None], scores, MASKED)
    sink_grid = sink_logits.reshape(kv_here, group_size, 1, 1)
    row_top = jnp.maximum(jnp.max(masked_scores, axis=-1, keepdims=True), sink_grid)
    expo_scores = jnp.where(allowed[None, None], jnp.exp(masked_scores - row_top), 0.0)
    denominator = jnp.sum(expo_scores, axis=-1, keepdims=True) + jnp.exp(sink_grid - row_top)
    attn_weights = (expo_scores / denominator).astype(BF16)
    mixed_heads = jnp.einsum(
        "cgqk,kcd->qcgd", attn_weights, values_all, preferred_element_type=F32
    )
    return mixed_heads.astype(BF16).reshape(seg_len, heads_here * HEAD_DIM)


def up_ring(block):
    n = lax.axis_size("exp")
    return lax.ppermute(block, "exp", [(i, (i + 1) % n) for i in range(n)])


def down_ring(block):
    n = lax.axis_size("exp")
    return lax.ppermute(block, "exp", [(i, (i - 1) % n) for i in range(n)])


def ring_sum(part_for):
    far = lax.axis_size("exp") // 2
    ahead = up_ring(part_for(far, 0).astype(BF16)).astype(F32)
    behind = down_ring(part_for(far, 1).astype(BF16)).astype(F32)
    rows = ahead.shape[0]
    ahead = jnp.pad(ahead, ((0, rows), (0, 0)))
    behind = jnp.pad(behind, ((rows, 0), (0, 0)))
    for distance in range(far - 1, 0, -1):
        ahead = up_ring((part_for(distance, None) + ahead).astype(BF16)).astype(F32)
        behind = down_ring((part_for(-distance, None) + behind).astype(BF16)).astype(F32)
    return part_for(0, None) + ahead + behind


def ring_visit(own, visit):
    far = lax.axis_size("exp") // 2
    own = with_layout_constraint(own, Layout((1, 0)))
    ahead = behind = own
    for distance in range(1, far):
        ahead = up_ring(ahead)
        behind = down_ring(behind)
        visit(1 - distance, own if distance == 1 else last[0])
        if distance > 1:
            visit(distance - 1, last[1])
        last = (ahead, behind)
    rows = own.shape[0] // 2
    ahead = up_ring(ahead[:rows])
    behind = down_ring(behind[rows:])
    visit(1 - far, last[0])
    visit(far - 1, last[1])
    visit(far, jnp.concatenate([ahead, behind], axis=0))


def two_stage_sum(chunks):
    n = lax.axis_size("exp")
    me = lax.axis_index("exp")
    pairs, odd = me // 2, lax.rem(me, 2)
    paired = chunks.reshape((n // 2, 2) + chunks.shape[1:])
    mine = lax.dynamic_index_in_dim(paired, odd, 1, keepdims=False)
    others = lax.dynamic_index_in_dim(paired, 1 - odd, 1, keepdims=False)
    swapped = lax.ppermute(others, "exp", [(i, i ^ 1) for i in range(n)])
    sums = mine.astype(F32) + swapped.astype(F32)
    total = lax.dynamic_index_in_dim(sums, pairs, 0, keepdims=False)
    sums = sums.astype(BF16)
    for distance in range(1, n // 2):
        share = lax.dynamic_index_in_dim(
            sums, lax.rem(pairs + distance, n // 2), 0, keepdims=False
        )
        route = [(i, (i + 2 * distance) % n) for i in range(n)]
        total = total + lax.ppermute(share, "exp", route).astype(F32)
    return total


def doubling_gather(own):
    n = lax.axis_size("exp")
    me = lax.axis_index("exp")
    blocks = own
    bit, depth = n // 2, 0
    while bit:
        other = lax.ppermute(blocks, "exp", [(i, i ^ bit) for i in range(n)])
        upper = (me & bit) != 0
        blocks = jnp.stack(
            [jnp.where(upper, other, blocks), jnp.where(upper, blocks, other)], axis=depth
        )
        bit, depth = bit // 2, depth + 1
    return blocks.reshape((n,) + own.shape)


def split_kernel(n_exp, w_ref, direct_ref, ring_ref):
    width = w_ref.shape[1] // n_exp
    ring = width - DIRECT
    for z in range(n_exp):
        block = w_ref[:, z * width : (z + 1) * width]
        direct_ref[:, z * DIRECT : (z + 1) * DIRECT] = block[:, :DIRECT]
        ring_ref[:, z * ring : (z + 1) * ring] = block[:, DIRECT:]


def split_columns(w, n_exp):
    rows, columns = w.shape
    direct = n_exp * DIRECT
    return pl.pallas_call(
        lambda *refs: split_kernel(n_exp, *refs),
        out_shape=(
            jax.ShapeDtypeStruct((rows, direct), BF16),
            jax.ShapeDtypeStruct((rows, columns - direct), BF16),
        ),
        compiler_params=pltpu.CompilerParams(vmem_limit_bytes=48 << 20),
        cost_estimate=pl.CostEstimate(
            flops=0, bytes_accessed=5 * rows * columns, transcendentals=0
        ),
        name="split_columns",
    )(w)


def stack_kernel(n_exp, w_ref, out_ref):
    width = w_ref.shape[1] // n_exp
    for z in range(n_exp):
        out_ref[z] = w_ref[:, z * width : (z + 1) * width]


def stack_columns(w, n_exp):
    rows, columns = w.shape
    return pl.pallas_call(
        lambda *refs: stack_kernel(n_exp, *refs),
        out_shape=jax.ShapeDtypeStruct((n_exp, rows, columns // n_exp), BF16),
        compiler_params=pltpu.CompilerParams(vmem_limit_bytes=48 << 20),
        cost_estimate=pl.CostEstimate(
            flops=0, bytes_accessed=5 * rows * columns, transcendentals=0
        ),
        name="stack_columns",
    )(w)


def grad_kernel(pairs, d_ref, direct_ref, ring_ref, out_ref):
    step = pl.program_id(0)
    d_value = d_ref[...]
    from_direct = jnp.dot(d_value, direct_ref[...], preferred_element_type=F32).astype(BF16)
    ring = ring_ref.shape[1]
    width = DIRECT + ring
    from_ring = [
        lax.dot_general(
            d_value, ring_ref[i], (((1,), (1,)), ((), ())), preferred_element_type=F32
        ).astype(BF16)
        for i in range(2)
    ]
    for pair in range(pairs):

        @pl.when(step == pair)
        def _():
            for i in range(2):
                first = (2 * pair + i) * width
                out_ref[:, first : first + DIRECT] = from_direct[
                    :, i * DIRECT : (i + 1) * DIRECT
                ]
                out_ref[:, first + DIRECT : first + width] = from_ring[i]


def grad_rows(d_value, direct_rows, ring_rows):
    n_exp, ring, slots = ring_rows.shape
    rows = d_value.shape[0]
    pairs = n_exp // 2
    return pl.pallas_call(
        lambda *refs: grad_kernel(pairs, *refs),
        out_shape=jax.ShapeDtypeStruct((rows, n_exp * (DIRECT + ring)), BF16),
        grid=(pairs,),
        in_specs=[
            pl.BlockSpec((rows, slots), lambda i: (0, 0)),
            pl.BlockSpec((slots, 2 * DIRECT), lambda i: (0, i)),
            pl.BlockSpec((2, ring, slots), lambda i: (i, 0, 0)),
        ],
        out_specs=pl.BlockSpec((rows, n_exp * (DIRECT + ring)), lambda i: (0, 0)),
        compiler_params=pltpu.CompilerParams(vmem_limit_bytes=48 << 20),
        name="grad_rows",
    )(d_value, direct_rows, ring_rows)


def over_seq(rows):
    n_seq = lax.axis_size("seq")
    blocks = rows.reshape(n_seq, rows.shape[0] // n_seq, rows.shape[1])
    return lax.all_to_all(blocks, "seq", split_axis=0, concat_axis=0, tiled=True).reshape(
        rows.shape
    )


def in_pieces(column):
    first = column.astype(BF16)
    second = (column - first.astype(F32)).astype(BF16)
    third = (column - first.astype(F32) - second.astype(F32)).astype(BF16)
    return [first, second, third]


def shards(
    queries,
    attn_keys,
    attn_values,
    sink_logits,
    out_proj,
    residual,
    norm_gain,
    doc_start,
    expert_ids,
    route_scores,
    w_gate_up,
    w_down,
    control,
):
    n_seq = lax.axis_size("seq")
    n_exp = lax.axis_size("exp")
    seg_len, width = residual.shape
    model = out_proj.shape[1]
    hid = w_down.shape[1]
    capacity = 2 * TOPK * seg_len // n_seq
    slots = n_seq * capacity
    me = lax.axis_index("exp")

    def chunk_at(distance):
        return lax.rem(me + distance + n_exp, n_exp)

    def pick(stacked, distance):
        return lax.dynamic_index_in_dim(stacked, chunk_at(distance), 0, keepdims=False)

    heads_out = attend(queries, attn_keys, attn_values, sink_logits, doc_start)
    partial_value = jnp.dot(heads_out, out_proj, preferred_element_type=F32).astype(BF16)
    partial_chunks = partial_value.reshape(seg_len, n_exp, width).transpose(1, 0, 2)

    mixed = two_stage_sum(partial_chunks) + residual.astype(F32)

    experts = jnp.arange(n_seq, dtype=jnp.int32)
    named = expert_ids[:, :, None] == experts[None, None, :]
    member = jnp.any(named, axis=1)
    route_gates = route_scores / jnp.sum(route_scores, axis=-1, keepdims=True)
    gate_table = jnp.sum(jnp.where(named, route_gates[:, :, None], 0.0), axis=1)
    position = jnp.arange(seg_len, dtype=jnp.int32)
    earlier = (position[:, None] > position[None, :]).astype(BF16)
    rank = jnp.dot(earlier, member.astype(BF16), preferred_element_type=F32)
    place = jnp.where(member, rank + 1.0, 0.0).astype(BF16)
    slot = jnp.arange(slots, dtype=jnp.int32)
    spread = (slot[None, :] // capacity == experts[:, None]).astype(BF16)
    place_wide = jnp.dot(place, spread, preferred_element_type=F32)
    taken = (place_wide == (slot % capacity + 1).astype(F32)[None, :]).astype(BF16)
    gate_wide = jnp.dot(gate_table, spread.astype(F32), precision=lax.Precision.HIGHEST)
    gate_slot = jnp.sum(taken.astype(F32) * gate_wide, axis=0)

    def to_slots(rows):
        return lax.dot_general(
            taken, rows, (((0,), (0,)), ((), ())), preferred_element_type=F32
        ).astype(BF16)

    ring = width - DIRECT

    def direct_rows(own, after):
        own, after = lax.optimization_barrier((own, after))
        gathered = doubling_gather(own)
        sent = to_slots(gathered.transpose(1, 0, 2).reshape(seg_len, n_exp * DIRECT))
        return over_seq(sent), after

    def ring_rows(own, visit=None):
        box = [jnp.zeros((n_exp, ring, slots), BF16)]

        def store(distance, chunk):
            box[0] = lax.dynamic_update_index_in_dim(
                box[0], chunk[:, :ring].T, chunk_at(distance), 0
            )
            if visit is not None:
                visit(chunk)

        ring_visit(own, store)
        return box[0]

    def weighted(split, direct, stacked):
        return lax.dot_general(
            split[0], direct, (((1,), (1,)), ((), ())), preferred_element_type=F32
        ) + jnp.dot(
            split[1], stacked.reshape(n_exp * ring, slots), preferred_element_type=F32
        )

    gain = lax.dynamic_slice_in_dim(norm_gain, me * width, width, 0)
    squares = jnp.sum(mixed * mixed, axis=1, keepdims=True)
    scaled = (mixed * gain[None, :]).astype(BF16)
    sent = jnp.concatenate(
        [to_slots(jnp.concatenate([scaled[:, DIRECT:]] + in_pieces(squares), axis=1))]
        + in_pieces(gate_slot[:, None]),
        axis=1,
    )
    up_weights = w_gate_up[0].transpose(0, 2, 1).reshape(2 * hid, model)
    up_weights, down_weights, sent = lax.optimization_barrier((up_weights, w_down[0], sent))
    up_split = split_columns(up_weights, n_exp)
    down_split = split_columns(down_weights, n_exp)
    down_stack = stack_columns(down_weights, n_exp)

    square_sums = []
    direct, sent = direct_rows(scaled[:, :DIRECT], sent)
    own_rows = over_seq(sent)
    gates = jnp.sum(own_rows[:, ring + 3 : ring + 6].astype(F32), axis=1)[None, :]
    stacked = ring_rows(
        own_rows,
        lambda chunk: square_sums.append(
            jnp.sum(chunk[:, ring : ring + 3].astype(F32), axis=1)
        ),
    )
    scale = lax.rsqrt(sum(square_sums) / model + EPSILON)[None, :]
    value = scale * weighted(up_split, direct, stacked)
    gate_value = value[:hid]
    up_value = value[hid:]
    squashed = jax.nn.sigmoid(GLU_ALPHA * gate_value)
    glu_value = gate_value * squashed
    hidden = (gates * ((up_value + 1.0) * glu_value)).astype(BF16).T

    def out_part(distance, half):
        count = slots // 2
        left = hidden if half is None else hidden[half * count : (half + 1) * count]
        return jnp.dot(left, pick(down_stack, distance), preferred_element_type=F32)

    returned = over_seq(ring_sum(out_part).astype(BF16))
    moe_out = jnp.dot(taken, returned, preferred_element_type=F32)
    target = STEER * control / jnp.sqrt(jnp.sum(control * control))
    own_target = lax.dynamic_slice_in_dim(target, me * width, width, 0)
    residual_error = (mixed + moe_out - own_target[None, :]).astype(BF16)

    sent = to_slots(residual_error[:, DIRECT:])
    direct_error, sent = direct_rows(residual_error[:, :DIRECT], sent)
    ring_error = ring_rows(over_seq(sent))
    d_hidden = (gates * scale) * weighted(down_split, direct_error, ring_error)
    d_gate = (
        d_hidden
        * (up_value + 1.0)
        * (squashed + GLU_ALPHA * gate_value * squashed * (1.0 - squashed))
    ).astype(BF16)
    d_up = (d_hidden * glu_value).astype(BF16)
    grads = grad_rows(jnp.concatenate([d_gate, d_up], axis=0), direct, stacked)
    return grads.reshape(1, 2, hid, model).transpose(0, 1, 3, 2)


def solution(mesh):
    return jax.shard_map(
        shards,
        mesh=mesh,
        in_specs=(
            P("seq", "exp"),
            P("seq", "exp"),
            P("seq", "exp"),
            P("exp"),
            P("exp", None),
            P("seq", "exp"),
            P(),
            P("seq"),
            P("seq", None),
            P("seq", None),
            P("seq", None, None, "exp"),
            P("seq", "exp", None),
            P(),
        ),
        out_specs=P("seq", None, None, "exp"),
        check_vma=False,
    )
```

```python
import jax
import jax.numpy as jnp
from jax import lax
from jax.experimental import pallas as pl
from jax.experimental.layout import Layout, with_layout_constraint
from jax.experimental.pallas import tpu as pltpu
from jax.sharding import PartitionSpec as P

HEAD_DIM = 64
WINDOW = 128
TOPK = 4
GLU_ALPHA = 1.702
STEER = 6.5
EPSILON = 1e-05
MASKED = -1e30
BF16 = jnp.bfloat16
F32 = jnp.float32
DIRECT = 128


def passed_along(block, axis, distance):
    devices = range(lax.axis_size(axis))
    route = [(i - distance, i) for i in devices if i - distance in devices]
    return lax.ppermute(block, axis, route)


def attend(queries, attn_keys, attn_values, sink_logits, doc_start):
    seg_len = queries.shape[0]
    heads_here = queries.shape[1] // HEAD_DIM
    kv_here = attn_keys.shape[1] // HEAD_DIM
    group_size = heads_here // kv_here
    both_rims = passed_along(jnp.stack([attn_keys, attn_values]), "seq", 1)
    keys_all = jnp.concatenate([both_rims[0], attn_keys], axis=0).reshape(
        WINDOW + seg_len, kv_here, HEAD_DIM
    )
    values_all = jnp.concatenate([both_rims[1], attn_values], axis=0).reshape(
        WINDOW + seg_len, kv_here, HEAD_DIM
    )
    offset = lax.axis_index("seq") * seg_len
    query_pos = offset + jnp.arange(seg_len, dtype=jnp.int32)
    key_pos = offset - WINDOW + jnp.arange(WINDOW + seg_len, dtype=jnp.int32)
    allowed = (
        (key_pos[None, :] <= query_pos[:, None])
        & (key_pos[None, :] > query_pos[:, None] - WINDOW)
        & (key_pos[None, :] >= doc_start[:, None])
    )
    grouped = queries.reshape(seg_len, kv_here, group_size, HEAD_DIM)
    scores = jnp.einsum(
        "qcgd,kcd->cgqk", grouped, keys_all, preferred_element_type=F32
    ) * HEAD_DIM ** (-0.5)
    masked_scores = jnp.where(allowed[None, None], scores, MASKED)
    sink_grid = sink_logits.reshape(kv_here, group_size, 1, 1)
    row_top = jnp.maximum(jnp.max(masked_scores, axis=-1, keepdims=True), sink_grid)
    expo_scores = jnp.where(allowed[None, None], jnp.exp(masked_scores - row_top), 0.0)
    denominator = jnp.sum(expo_scores, axis=-1, keepdims=True) + jnp.exp(sink_grid - row_top)
    attn_weights = (expo_scores / denominator).astype(BF16)
    mixed_heads = jnp.einsum(
        "cgqk,kcd->qcgd", attn_weights, values_all, preferred_element_type=F32
    )
    return mixed_heads.astype(BF16).reshape(seg_len, heads_here * HEAD_DIM)


def up_ring(block):
    n = lax.axis_size("exp")
    return lax.ppermute(block, "exp", [(i, (i + 1) % n) for i in range(n)])


def down_ring(block):
    n = lax.axis_size("exp")
    return lax.ppermute(block, "exp", [(i, (i - 1) % n) for i in range(n)])


def ring_sum(part_for):
    far = lax.axis_size("exp") // 2
    ahead = up_ring(part_for(far, 0).astype(BF16)).astype(F32)
    behind = down_ring(part_for(far, 1).astype(BF16)).astype(F32)
    rows = ahead.shape[0]
    ahead = jnp.pad(ahead, ((0, rows), (0, 0)))
    behind = jnp.pad(behind, ((rows, 0), (0, 0)))
    for distance in range(far - 1, 0, -1):
        ahead = up_ring((part_for(distance, None) + ahead).astype(BF16)).astype(F32)
        behind = down_ring((part_for(-distance, None) + behind).astype(BF16)).astype(F32)
    return part_for(0, None) + ahead + behind


def ring_visit(own, visit):
    far = lax.axis_size("exp") // 2
    own = with_layout_constraint(own, Layout((1, 0)))
    ahead = behind = own
    for distance in range(1, far):
        ahead = up_ring(ahead)
        behind = down_ring(behind)
        visit(1 - distance, own if distance == 1 else last[0])
        if distance > 1:
            visit(distance - 1, last[1])
        last = (ahead, behind)
    rows = own.shape[0] // 2
    ahead = up_ring(ahead[:rows])
    behind = down_ring(behind[rows:])
    visit(1 - far, last[0])
    visit(far - 1, last[1])
    visit(far, jnp.concatenate([ahead, behind], axis=0))


def two_stage_sum(chunks):
    n = lax.axis_size("exp")
    me = lax.axis_index("exp")
    pairs, odd = me // 2, lax.rem(me, 2)
    paired = chunks.reshape((n // 2, 2) + chunks.shape[1:])
    mine = lax.dynamic_index_in_dim(paired, odd, 1, keepdims=False)
    others = lax.dynamic_index_in_dim(paired, 1 - odd, 1, keepdims=False)
    swapped = lax.ppermute(others, "exp", [(i, i ^ 1) for i in range(n)])
    sums = mine.astype(F32) + swapped.astype(F32)
    total = lax.dynamic_index_in_dim(sums, pairs, 0, keepdims=False)
    sums = sums.astype(BF16)
    for distance in range(1, n // 2):
        share = lax.dynamic_index_in_dim(
            sums, lax.rem(pairs + distance, n // 2), 0, keepdims=False
        )
        route = [(i, (i + 2 * distance) % n) for i in range(n)]
        total = total + lax.ppermute(share, "exp", route).astype(F32)
    return total


def doubling_gather(own):
    n = lax.axis_size("exp")
    me = lax.axis_index("exp")
    blocks = own
    bit, depth = n // 2, 0
    while bit:
        other = lax.ppermute(blocks, "exp", [(i, i ^ bit) for i in range(n)])
        upper = (me & bit) != 0
        blocks = jnp.stack(
            [jnp.where(upper, other, blocks), jnp.where(upper, blocks, other)], axis=depth
        )
        bit, depth = bit // 2, depth + 1
    return blocks.reshape((n,) + own.shape)


def split_kernel(n_exp, w_ref, direct_ref, ring_ref):
    width = w_ref.shape[1] // n_exp
    ring = width - DIRECT
    for z in range(n_exp):
        block = w_ref[:, z * width : (z + 1) * width]
        direct_ref[:, z * DIRECT : (z + 1) * DIRECT] = block[:, :DIRECT]
        ring_ref[:, z * ring : (z + 1) * ring] = block[:, DIRECT:]


def split_columns(w, n_exp):
    rows, columns = w.shape
    direct = n_exp * DIRECT
    return pl.pallas_call(
        lambda *refs: split_kernel(n_exp, *refs),
        out_shape=(
            jax.ShapeDtypeStruct((rows, direct), BF16),
            jax.ShapeDtypeStruct((rows, columns - direct), BF16),
        ),
        compiler_params=pltpu.CompilerParams(vmem_limit_bytes=48 << 20),
        cost_estimate=pl.CostEstimate(
            flops=0, bytes_accessed=5 * rows * columns, transcendentals=0
        ),
        name="split_columns",
    )(w)


def stack_kernel(n_exp, w_ref, out_ref):
    width = w_ref.shape[1] // n_exp
    for z in range(n_exp):
        out_ref[z] = w_ref[:, z * width : (z + 1) * width]


def stack_columns(w, n_exp):
    rows, columns = w.shape
    return pl.pallas_call(
        lambda *refs: stack_kernel(n_exp, *refs),
        out_shape=jax.ShapeDtypeStruct((n_exp, rows, columns // n_exp), BF16),
        compiler_params=pltpu.CompilerParams(vmem_limit_bytes=48 << 20),
        cost_estimate=pl.CostEstimate(
            flops=0, bytes_accessed=5 * rows * columns, transcendentals=0
        ),
        name="stack_columns",
    )(w)


def grad_kernel(pairs, d_ref, direct_ref, ring_ref, out_ref):
    step = pl.program_id(0)
    d_value = d_ref[...]
    from_direct = jnp.dot(d_value, direct_ref[...], preferred_element_type=F32).astype(BF16)
    ring = ring_ref.shape[1]
    width = DIRECT + ring
    from_ring = [
        lax.dot_general(
            d_value, ring_ref[i], (((1,), (1,)), ((), ())), preferred_element_type=F32
        ).astype(BF16)
        for i in range(2)
    ]
    for pair in range(pairs):

        @pl.when(step == pair)
        def _():
            for i in range(2):
                first = (2 * pair + i) * width
                out_ref[:, first : first + DIRECT] = from_direct[
                    :, i * DIRECT : (i + 1) * DIRECT
                ]
                out_ref[:, first + DIRECT : first + width] = from_ring[i]


def grad_rows(d_value, direct_rows, ring_rows):
    n_exp, ring, slots = ring_rows.shape
    rows = d_value.shape[0]
    pairs = n_exp // 2
    return pl.pallas_call(
        lambda *refs: grad_kernel(pairs, *refs),
        out_shape=jax.ShapeDtypeStruct((rows, n_exp * (DIRECT + ring)), BF16),
        grid=(pairs,),
        in_specs=[
            pl.BlockSpec((rows, slots), lambda i: (0, 0)),
            pl.BlockSpec((slots, 2 * DIRECT), lambda i: (0, i)),
            pl.BlockSpec((2, ring, slots), lambda i: (i, 0, 0)),
        ],
        out_specs=pl.BlockSpec((rows, n_exp * (DIRECT + ring)), lambda i: (0, 0)),
        compiler_params=pltpu.CompilerParams(vmem_limit_bytes=48 << 20),
        name="grad_rows",
    )(d_value, direct_rows, ring_rows)


def over_seq(rows):
    n_seq = lax.axis_size("seq")
    blocks = rows.reshape(n_seq, rows.shape[0] // n_seq, rows.shape[1])
    return lax.all_to_all(blocks, "seq", split_axis=0, concat_axis=0, tiled=True).reshape(
        rows.shape
    )


def in_pieces(column):
    first = column.astype(BF16)
    second = (column - first.astype(F32)).astype(BF16)
    third = (column - first.astype(F32) - second.astype(F32)).astype(BF16)
    return [first, second, third]


def shards(
    queries,
    attn_keys,
    attn_values,
    sink_logits,
    out_proj,
    residual,
    norm_gain,
    doc_start,
    expert_ids,
    route_scores,
    w_gate_up,
    w_down,
    control,
):
    n_seq = lax.axis_size("seq")
    n_exp = lax.axis_size("exp")
    seg_len, width = residual.shape
    model = out_proj.shape[1]
    hid = w_down.shape[1]
    capacity = 2 * TOPK * seg_len // n_seq
    slots = n_seq * capacity
    me = lax.axis_index("exp")

    def chunk_at(distance):
        return lax.rem(me + distance + n_exp, n_exp)

    def pick(stacked, distance):
        return lax.dynamic_index_in_dim(stacked, chunk_at(distance), 0, keepdims=False)

    heads_out = attend(queries, attn_keys, attn_values, sink_logits, doc_start)
    partial_value = jnp.dot(heads_out, out_proj, preferred_element_type=F32).astype(BF16)
    partial_chunks = partial_value.reshape(seg_len, n_exp, width).transpose(1, 0, 2)

    mixed = two_stage_sum(partial_chunks) + residual.astype(F32)

    experts = jnp.arange(n_seq, dtype=jnp.int32)
    named = expert_ids[:, :, None] == experts[None, None, :]
    member = jnp.any(named, axis=1)
    route_gates = route_scores / jnp.sum(route_scores, axis=-1, keepdims=True)
    gate_table = jnp.sum(jnp.where(named, route_gates[:, :, None], 0.0), axis=1)
    position = jnp.arange(seg_len, dtype=jnp.int32)
    earlier = (position[:, None] > position[None, :]).astype(BF16)
    rank = jnp.dot(earlier, member.astype(BF16), preferred_element_type=F32)
    place = jnp.where(member, rank + 1.0, 0.0).astype(BF16)
    slot = jnp.arange(slots, dtype=jnp.int32)
    spread = (slot[None, :] // capacity == experts[:, None]).astype(BF16)
    place_wide = jnp.dot(place, spread, preferred_element_type=F32)
    taken = (place_wide == (slot % capacity + 1).astype(F32)[None, :]).astype(BF16)
    gate_wide = jnp.dot(gate_table, spread.astype(F32), precision=lax.Precision.HIGHEST)
    gate_slot = jnp.sum(taken.astype(F32) * gate_wide, axis=0)

    def to_slots(rows):
        return lax.dot_general(
            taken, rows, (((0,), (0,)), ((), ())), preferred_element_type=F32
        ).astype(BF16)

    ring = width - DIRECT

    def direct_rows(own, after):
        own, after = lax.optimization_barrier((own, after))
        gathered = doubling_gather(own)
        sent = to_slots(gathered.transpose(1, 0, 2).reshape(seg_len, n_exp * DIRECT))
        return over_seq(sent), after

    def ring_rows(own, visit=None):
        box = [jnp.zeros((n_exp, ring, slots), BF16)]

        def store(distance, chunk):
            box[0] = lax.dynamic_update_index_in_dim(
                box[0], chunk[:, :ring].T, chunk_at(distance), 0
            )
            if visit is not None:
                visit(chunk)

        ring_visit(own, store)
        return box[0]

    def weighted(split, direct, stacked):
        return lax.dot_general(
            split[0], direct, (((1,), (1,)), ((), ())), preferred_element_type=F32
        ) + jnp.dot(
            split[1], stacked.reshape(n_exp * ring, slots), preferred_element_type=F32
        )

    gain = lax.dynamic_slice_in_dim(norm_gain, me * width, width, 0)
    squares = jnp.sum(mixed * mixed, axis=1, keepdims=True)
    scaled = (mixed * gain[None, :]).astype(BF16)
    sent = jnp.concatenate(
        [to_slots(jnp.concatenate([scaled[:, DIRECT:]] + in_pieces(squares), axis=1))]
        + in_pieces(gate_slot[:, None]),
        axis=1,
    )
    up_weights = w_gate_up[0].transpose(0, 2, 1).reshape(2 * hid, model)
    up_weights, down_weights, sent = lax.optimization_barrier((up_weights, w_down[0], sent))
    up_split = split_columns(up_weights, n_exp)
    down_split = split_columns(down_weights, n_exp)
    down_stack = stack_columns(down_weights, n_exp)

    square_sums = []
    direct, own_rows = direct_rows(scaled[:, :DIRECT], over_seq(sent))
    gates = jnp.sum(own_rows[:, ring + 3 : ring + 6].astype(F32), axis=1)[None, :]
    stacked = ring_rows(
        own_rows,
        lambda chunk: square_sums.append(
            jnp.sum(chunk[:, ring : ring + 3].astype(F32), axis=1)
        ),
    )
    scale = lax.rsqrt(sum(square_sums) / model + EPSILON)[None, :]
    value = scale * weighted(up_split, direct, stacked)
    gate_value = value[:hid]
    up_value = value[hid:]
    squashed = jax.nn.sigmoid(GLU_ALPHA * gate_value)
    glu_value = gate_value * squashed
    hidden = (gates * ((up_value + 1.0) * glu_value)).astype(BF16).T

    def out_part(distance, half):
        count = slots // 2
        left = hidden if half is None else hidden[half * count : (half + 1) * count]
        return jnp.dot(left, pick(down_stack, distance), preferred_element_type=F32)

    returned = over_seq(ring_sum(out_part).astype(BF16))
    moe_out = jnp.dot(taken, returned, preferred_element_type=F32)
    target = STEER * control / jnp.sqrt(jnp.sum(control * control))
    own_target = lax.dynamic_slice_in_dim(target, me * width, width, 0)
    residual_error = (mixed + moe_out - own_target[None, :]).astype(BF16)

    own_error = over_seq(to_slots(residual_error[:, DIRECT:]))
    direct_error, own_error = direct_rows(residual_error[:, :DIRECT], own_error)
    ring_error = ring_rows(own_error)
    d_hidden = (gates * scale) * weighted(down_split, direct_error, ring_error)
    d_gate = (
        d_hidden
        * (up_value + 1.0)
        * (squashed + GLU_ALPHA * gate_value * squashed * (1.0 - squashed))
    ).astype(BF16)
    d_up = (d_hidden * glu_value).astype(BF16)
    grads = grad_rows(jnp.concatenate([d_gate, d_up], axis=0), direct, stacked)
    return grads.reshape(1, 2, hid, model).transpose(0, 1, 3, 2)


def solution(mesh):
    return jax.shard_map(
        shards,
        mesh=mesh,
        in_specs=(
            P("seq", "exp"),
            P("seq", "exp"),
            P("seq", "exp"),
            P("exp"),
            P("exp", None),
            P("seq", "exp"),
            P(),
            P("seq"),
            P("seq", None),
            P("seq", None),
            P("seq", None, None, "exp"),
            P("seq", "exp", None),
            P(),
        ),
        out_specs=P("seq", None, None, "exp"),
        check_vma=False,
    )
```

```python
import jax
import jax.numpy as jnp
from jax import lax
from jax.experimental import pallas as pl
from jax.experimental.layout import Layout, with_layout_constraint
from jax.experimental.pallas import tpu as pltpu
from jax.sharding import PartitionSpec as P

HEAD_DIM = 64
WINDOW = 128
TOPK = 4
GLU_ALPHA = 1.702
STEER = 6.5
EPSILON = 1e-05
MASKED = -1e30
BF16 = jnp.bfloat16
F32 = jnp.float32
GRAD_BLOCK = 768


def passed_along(block, axis, distance):
    devices = range(lax.axis_size(axis))
    route = [(i - distance, i) for i in devices if i - distance in devices]
    return lax.ppermute(block, axis, route)


def attend(queries, attn_keys, attn_values, sink_logits, doc_start):
    seg_len = queries.shape[0]
    heads_here = queries.shape[1] // HEAD_DIM
    kv_here = attn_keys.shape[1] // HEAD_DIM
    group_size = heads_here // kv_here
    both_rims = passed_along(jnp.stack([attn_keys, attn_values]), "seq", 1)
    keys_all = jnp.concatenate([both_rims[0], attn_keys], axis=0).reshape(
        WINDOW + seg_len, kv_here, HEAD_DIM
    )
    values_all = jnp.concatenate([both_rims[1], attn_values], axis=0).reshape(
        WINDOW + seg_len, kv_here, HEAD_DIM
    )
    offset = lax.axis_index("seq") * seg_len
    query_pos = offset + jnp.arange(seg_len, dtype=jnp.int32)
    key_pos = offset - WINDOW + jnp.arange(WINDOW + seg_len, dtype=jnp.int32)
    allowed = (
        (key_pos[None, :] <= query_pos[:, None])
        & (key_pos[None, :] > query_pos[:, None] - WINDOW)
        & (key_pos[None, :] >= doc_start[:, None])
    )
    grouped = queries.reshape(seg_len, kv_here, group_size, HEAD_DIM)
    scores = jnp.einsum(
        "qcgd,kcd->cgqk", grouped, keys_all, preferred_element_type=F32
    ) * HEAD_DIM ** (-0.5)
    masked_scores = jnp.where(allowed[None, None], scores, MASKED)
    sink_grid = sink_logits.reshape(kv_here, group_size, 1, 1)
    row_top = jnp.maximum(jnp.max(masked_scores, axis=-1, keepdims=True), sink_grid)
    expo_scores = jnp.where(allowed[None, None], jnp.exp(masked_scores - row_top), 0.0)
    denominator = jnp.sum(expo_scores, axis=-1, keepdims=True) + jnp.exp(sink_grid - row_top)
    attn_weights = (expo_scores / denominator).astype(BF16)
    mixed_heads = jnp.einsum(
        "cgqk,kcd->qcgd", attn_weights, values_all, preferred_element_type=F32
    )
    return mixed_heads.astype(BF16).reshape(seg_len, heads_here * HEAD_DIM)


def up_ring(block):
    n = lax.axis_size("exp")
    return lax.ppermute(block, "exp", [(i, (i + 1) % n) for i in range(n)])


def down_ring(block):
    n = lax.axis_size("exp")
    return lax.ppermute(block, "exp", [(i, (i - 1) % n) for i in range(n)])


def ring_sum(part_for):
    far = lax.axis_size("exp") // 2
    ahead = up_ring(part_for(far, 0).astype(BF16)).astype(F32)
    behind = down_ring(part_for(far, 1).astype(BF16)).astype(F32)
    rows = ahead.shape[0]
    ahead = jnp.pad(ahead, ((0, rows), (0, 0)))
    behind = jnp.pad(behind, ((rows, 0), (0, 0)))
    for distance in range(far - 1, 0, -1):
        ahead = up_ring((part_for(distance, None) + ahead).astype(BF16)).astype(F32)
        behind = down_ring((part_for(-distance, None) + behind).astype(BF16)).astype(F32)
    return part_for(0, None) + ahead + behind


def ring_visit(own, visit):
    far = lax.axis_size("exp") // 2
    own = with_layout_constraint(own, Layout((1, 0)))
    ahead = behind = own
    for distance in range(1, far):
        ahead = up_ring(ahead)
        behind = down_ring(behind)
        visit(1 - distance, own if distance == 1 else last[0])
        if distance > 1:
            visit(distance - 1, last[1])
        last = (ahead, behind)
    rows = own.shape[0] // 2
    ahead = up_ring(ahead[:rows])
    behind = down_ring(behind[rows:])
    visit(1 - far, last[0])
    visit(far - 1, last[1])
    visit(far, jnp.concatenate([ahead, behind], axis=0))


def two_stage_sum(chunks):
    n = lax.axis_size("exp")
    me = lax.axis_index("exp")
    pairs, odd = me // 2, lax.rem(me, 2)
    paired = chunks.reshape((n // 2, 2) + chunks.shape[1:])
    mine = lax.dynamic_index_in_dim(paired, odd, 1, keepdims=False)
    others = lax.dynamic_index_in_dim(paired, 1 - odd, 1, keepdims=False)
    swapped = lax.ppermute(others, "exp", [(i, i ^ 1) for i in range(n)])
    sums = mine.astype(F32) + swapped.astype(F32)
    total = lax.dynamic_index_in_dim(sums, pairs, 0, keepdims=False)
    sums = sums.astype(BF16)
    for distance in range(1, n // 2):
        share = lax.dynamic_index_in_dim(
            sums, lax.rem(pairs + distance, n // 2), 0, keepdims=False
        )
        route = [(i, (i + 2 * distance) % n) for i in range(n)]
        total = total + lax.ppermute(share, "exp", route).astype(F32)
    return total


def split_kernel(n_exp, w_ref, out_ref):
    width = w_ref.shape[1] // n_exp
    for z in range(n_exp):
        out_ref[z] = w_ref[:, z * width : (z + 1) * width]


def split_columns(w, n_exp):
    rows, columns = w.shape
    return pl.pallas_call(
        lambda *refs: split_kernel(n_exp, *refs),
        out_shape=jax.ShapeDtypeStruct((n_exp, rows, columns // n_exp), BF16),
        compiler_params=pltpu.CompilerParams(vmem_limit_bytes=48 << 20),
        cost_estimate=pl.CostEstimate(
            flops=0, bytes_accessed=5 * rows * columns, transcendentals=0
        ),
        name="split_columns",
    )(w)


def grad_kernel(d_ref, rows_ref, out_ref):
    out_ref[...] = lax.dot_general(
        d_ref[...], rows_ref[...], (((1,), (1,)), ((), ())), preferred_element_type=F32
    ).astype(BF16)


def grad_rows(d_value, rows):
    count, slots = d_value.shape
    model = rows.shape[0]
    block = min(GRAD_BLOCK, model)
    return pl.pallas_call(
        grad_kernel,
        out_shape=jax.ShapeDtypeStruct((count, model), BF16),
        grid=(pl.cdiv(model, block),),
        in_specs=[
            pl.BlockSpec((count, slots), lambda i: (0, 0)),
            pl.BlockSpec((block, slots), lambda i: (i, 0)),
        ],
        out_specs=pl.BlockSpec((count, block), lambda i: (0, i)),
        compiler_params=pltpu.CompilerParams(vmem_limit_bytes=48 << 20),
        name="grad_rows",
    )(d_value, rows)


def over_seq(rows):
    n_seq = lax.axis_size("seq")
    blocks = rows.reshape(n_seq, rows.shape[0] // n_seq, rows.shape[1])
    return lax.all_to_all(blocks, "seq", split_axis=0, concat_axis=0, tiled=True).reshape(
        rows.shape
    )


def in_pieces(column):
    first = column.astype(BF16)
    second = (column - first.astype(F32)).astype(BF16)
    third = (column - first.astype(F32) - second.astype(F32)).astype(BF16)
    return [first, second, third]


def shards(
    queries,
    attn_keys,
    attn_values,
    sink_logits,
    out_proj,
    residual,
    norm_gain,
    doc_start,
    expert_ids,
    route_scores,
    w_gate_up,
    w_down,
    control,
):
    n_seq = lax.axis_size("seq")
    n_exp = lax.axis_size("exp")
    seg_len, width = residual.shape
    model = out_proj.shape[1]
    hid = w_down.shape[1]
    capacity = 2 * TOPK * seg_len // n_seq
    slots = n_seq * capacity
    me = lax.axis_index("exp")

    def chunk_at(distance):
        return lax.rem(me + distance + n_exp, n_exp)

    def pick(stacked, distance):
        return lax.dynamic_index_in_dim(stacked, chunk_at(distance), 0, keepdims=False)

    heads_out = attend(queries, attn_keys, attn_values, sink_logits, doc_start)
    partial_value = jnp.dot(heads_out, out_proj, preferred_element_type=F32).astype(BF16)
    partial_chunks = partial_value.reshape(seg_len, n_exp, width).transpose(1, 0, 2)

    partial_chunks, expert_ids, route_scores = lax.optimization_barrier(
        (partial_chunks, expert_ids, route_scores)
    )
    mixed = two_stage_sum(partial_chunks) + residual.astype(F32)

    experts = jnp.arange(n_seq, dtype=jnp.int32)
    named = expert_ids[:, :, None] == experts[None, None, :]
    member = jnp.any(named, axis=1)
    route_gates = route_scores / jnp.sum(route_scores, axis=-1, keepdims=True)
    gate_table = jnp.sum(jnp.where(named, route_gates[:, :, None], 0.0), axis=1)
    position = jnp.arange(seg_len, dtype=jnp.int32)
    earlier = (position[:, None] > position[None, :]).astype(BF16)
    rank = jnp.dot(earlier, member.astype(BF16), preferred_element_type=F32)
    place = jnp.where(member, rank + 1.0, 0.0).astype(BF16)
    slot = jnp.arange(slots, dtype=jnp.int32)
    spread = (slot[None, :] // capacity == experts[:, None]).astype(BF16)
    place_wide = jnp.dot(place, spread, preferred_element_type=F32)
    taken = (place_wide == (slot % capacity + 1).astype(F32)[None, :]).astype(BF16)
    gate_wide = jnp.dot(gate_table, spread.astype(F32), precision=lax.Precision.HIGHEST)
    gate_slot = jnp.sum(taken.astype(F32) * gate_wide, axis=0)

    def to_slots(rows):
        return lax.dot_general(
            taken, rows, (((0,), (0,)), ((), ())), preferred_element_type=F32
        ).astype(BF16)

    gain = lax.dynamic_slice_in_dim(norm_gain, me * width, width, 0)
    squares = jnp.sum(mixed * mixed, axis=1, keepdims=True)
    scaled = (mixed * gain[None, :]).astype(BF16)
    sent = jnp.concatenate(
        [to_slots(jnp.concatenate([scaled] + in_pieces(squares), axis=1))]
        + in_pieces(gate_slot[:, None]),
        axis=1,
    )
    down, sent = lax.optimization_barrier((w_down[0], sent))
    down_stack = split_columns(down, n_exp)

    def all_rows(own, visit=None):
        box = [jnp.zeros((n_exp, width, slots), BF16)]

        def store(distance, chunk):
            box[0] = lax.dynamic_update_index_in_dim(
                box[0], chunk[:, :width].T, chunk_at(distance), 0
            )
            if visit is not None:
                visit(chunk)

        ring_visit(own, store)
        return box[0].reshape(model, slots)

    square_sums = []
    own_rows = over_seq(sent)
    gates = jnp.sum(own_rows[:, width + 3 : width + 6].astype(F32), axis=1)[None, :]
    rows = all_rows(
        own_rows,
        lambda chunk: square_sums.append(
            jnp.sum(chunk[:, width : width + 3].astype(F32), axis=1)
        ),
    )
    scale = lax.rsqrt(sum(square_sums) / model + EPSILON)[None, :]
    up_weights = w_gate_up[0].transpose(0, 2, 1).reshape(2 * hid, model)
    value = scale * jnp.dot(up_weights, rows, preferred_element_type=F32)
    gate_value = value[:hid]
    up_value = value[hid:]
    squashed = jax.nn.sigmoid(GLU_ALPHA * gate_value)
    glu_value = gate_value * squashed
    hidden = (gates * ((up_value + 1.0) * glu_value)).astype(BF16).T

    def out_part(distance, half):
        count = slots // 2
        left = hidden if half is None else hidden[half * count : (half + 1) * count]
        return jnp.dot(left, pick(down_stack, distance), preferred_element_type=F32)

    returned = over_seq(ring_sum(out_part).astype(BF16))
    moe_out = jnp.dot(taken, returned, preferred_element_type=F32)
    target = STEER * control / jnp.sqrt(jnp.sum(control * control))
    own_target = lax.dynamic_slice_in_dim(target, me * width, width, 0)
    residual_error = (mixed + moe_out - own_target[None, :]).astype(BF16)

    error_rows = all_rows(over_seq(to_slots(residual_error)))
    d_hidden = (gates * scale) * jnp.dot(w_down[0], error_rows, preferred_element_type=F32)
    d_gate = (
        d_hidden
        * (up_value + 1.0)
        * (squashed + GLU_ALPHA * gate_value * squashed * (1.0 - squashed))
    ).astype(BF16)
    d_up = (d_hidden * glu_value).astype(BF16)
    grads = grad_rows(jnp.concatenate([d_gate, d_up], axis=0), rows)
    return grads.reshape(1, 2, hid, model).transpose(0, 1, 3, 2)


def solution(mesh):
    return jax.shard_map(
        shards,
        mesh=mesh,
        in_specs=(
            P("seq", "exp"),
            P("seq", "exp"),
            P("seq", "exp"),
            P("exp"),
            P("exp", None),
            P("seq", "exp"),
            P(),
            P("seq"),
            P("seq", None),
            P("seq", None),
            P("seq", None, None, "exp"),
            P("seq", "exp", None),
            P(),
        ),
        out_specs=P("seq", None, None, "exp"),
        check_vma=False,
    )
```
